128 devices in a mesh: dp: 32 (over y, x, core), head: 4 (over z).
Axes of the slice: x: 4, y: 4, z: 4, core: 2. Of those that a mesh axis runs over, the one named last changes fastest.
Arguments:
- queries: bfloat16 [2048, 8192], P('dp', 'head'), as said below
- new_keys: bfloat16 [2048, 512], P('dp', 'head'), may hold values from -6 to 6
- new_values: bfloat16 [2048, 512], P('dp', 'head'), may hold values from -6 to 6
- key_cache: bfloat16 [2048, 4, 256, 128], P('dp', 'head'), may hold values from -6 to 6
- value_cache: bfloat16 [2048, 4, 256, 128], P('dp', 'head'), may hold values from -6 to 6
- cache_lengths: int32 [2048], P('dp'), may hold values from 1 to 256, as said below
- out_weight: bfloat16 [8192, 4096], P('head', 'dp'), may hold values from -0.0625 to 0.0625
- residual_in: bfloat16 [2048, 4096], P(('dp', 'head')), may hold values from -6 to 6
- norm_gain: float32 [4096], replicated, may hold values from 0.25 to 1.75
- expert_ids: int32 [2048, 8], P(('dp', 'head')), may hold values from 0 to 63, all different within a row; in each aligned block of 16 rows (0 to 15, 16 to 31, ...) at most 4 rows name the same one
- route_weights: float32 [2048, 8], P(('dp', 'head')), may hold values from 0.05 to 1
- w_gate: bfloat16 [64, 4096, 1536], P('dp', None, 'head'), may hold values from -0.09375 to 0.09375
- w_up: bfloat16 [64, 4096, 1536], P('dp', None, 'head'), may hold values from -0.09375 to 0.09375
- w_down: bfloat16 [64, 1536, 4096], P('dp', 'head'), may hold values from -0.15625 to 0.15625
Outputs:
- layer_out: bfloat16 [2048, 4096], P(('dp', 'head'))
The draws below stay inside these ranges and needn't reach their ends.
Inputs may be any that keep to these rules, and one draw needn't show every extreme that they name: Each row's queries are real-valued; scores may be large. `cache_lengths`: at least one row in every draw has all 256 slots live. `expert_ids`: each row names 8 different experts; among the 16 rows of one device no expert is named by more than 4 rows.
All inputs are finite; a program needn't handle non-finite values.
Results may differ from the reference program's by a relative error of at most 0.0065.
Values may be sent and summed in bfloat16 or wider, within the bound.
A program may use at most 192 MiB of HBM per device.

```python
import math
import jax
import jax.numpy as jnp
import numpy as np
from jax import lax

D = 4096
H = 64
KVH = 4
HD = 128
EXPERTS = 64
FFW = 1536
TOPK = 8
ROW_DEV = 64
CAP = 256
ROWS = 2048
ROW_SHARD = 16
CAPY = 4


def draw_queries(key, part):
    key = jax.random.fold_in(key, 11)
    first = jax.random.fold_in(key, 0)
    base = jax.random.normal(first, (ROWS, H, HD), jnp.float32)
    return base.reshape(ROWS, H * HD).astype(jnp.bfloat16)


def draw_cache_lengths(key, part):
    key = jax.random.fold_in(key, 23)
    first, second, third = jax.random.split(key, 3)
    left = jax.random.randint(first, (ROWS,), 0, CAP)
    right = jax.random.randint(second, (ROWS,), 0, CAP)
    lengths = 1 + left * right // CAP
    chosen = jax.random.randint(third, (), 0, ROWS)
    lengths = jnp.where(jnp.arange(ROWS) == chosen, CAP, lengths)
    return lengths.astype(jnp.int32)


def shard_levels(own_key, dims, cuts, smallest, high):
    loudness = 1.0
    for axis_at, shards_of in cuts:
        heights = jax.random.uniform(jax.random.fold_in(jax.random.fold_in(own_key, 6), axis_at), (shards_of,), jnp.float32, smallest / len(cuts), high / len(cuts))
        loudness = loudness * jnp.repeat(jnp.exp(heights), dims[axis_at] // shards_of).reshape((-1,) + (1,) * (len(dims) - 1 - axis_at))
    return loudness


def routed_block(stream_key, own, number, rows, amount, top, limit, lean):
    sequence = jax.random.permutation(stream_key, amount)
    heavy_load, common = load_shares(amount, rows * top, limit, lean, True), load_shares(amount, rows * top, limit, lean, False)
    places = jnp.arange(amount)

    def named(sizes, offset_by):
        used = int((sizes > 0).sum())
        fixed = max(1, used // 4)
        moved = fixed + (places - fixed + offset_by * (used - fixed)) % max(1, amount - fixed)
        return jnp.zeros((amount,), jnp.int32).at[sequence[jnp.where(places < fixed, places, moved)]].set(jnp.asarray(sizes, jnp.int32))

    sizes = jnp.where(number % 4 == 0, named(heavy_load, number // 4), named(common, number - number // 4 - 1))
    mixed = jax.random.permutation(jax.random.fold_in(own, 3), amount)
    donor, sink = mixed[0:amount // 2 * 2:2], mixed[1:amount // 2 * 2:2]
    slack = jnp.minimum(sizes[donor] - 1, limit - sizes[sink]) // 2
    slack = jnp.where((donor == sequence[0]) | (sink == sequence[0]) | (sizes[sink] == 0), 0, jnp.maximum(slack, 0))
    moved = jax.random.randint(jax.random.fold_in(own, 4), (amount // 2,), 0, 1 << 20) % (slack + 1)
    sizes = sizes.at[donor].add(-moved).at[sink].add(moved)
    items = jnp.searchsorted(jnp.cumsum(sizes), jnp.arange(rows * top), side="right").astype(jnp.int32)
    grid = items.reshape(top, rows).T
    grid = grid[jax.random.permutation(jax.random.fold_in(own, 1), rows)]
    offset_by = jax.random.randint(jax.random.fold_in(own, 2), (rows, 1), 0, top)
    return jnp.take_along_axis(grid, (jnp.arange(top)[None, :] + offset_by) % top, axis=1)


def load_shares(number_of, total, limit, skew, full):
    weights = [(1 << 20) // math.isqrt(grade ** skew) + 1 for grade in range(1, number_of + 1)]
    largest = limit if full else min(limit, max(-(-total // number_of), total * weights[0] // sum(weights)))
    least = 1 if total - largest >= number_of - 1 else 0
    given, spare = [largest] + [least] * (number_of - 1), total - largest - least * (number_of - 1)
    while spare > 0:
        movable = [i for i in range(1, number_of) if given[i] < largest] or [i for i in range(1, number_of) if given[i] < limit]
        pool, remaining = sum([weights[i] for i in movable]), spare
        for i in movable:
            more = min(limit - given[i], max(1, remaining * weights[i] // pool), spare)
            given[i] = given[i] + more
            spare = spare - more
    return np.array(given)


def gaussian(stream_key, extent, scale, reach, cuts=(), kind=jnp.bfloat16):
    values = jax.random.normal(stream_key, extent, jnp.float32) * scale
    if len(cuts) > 0:
        values = shard_levels(stream_key, extent, cuts, -0.22, 0.18) * values
    return jnp.clip(values, min=-reach, max=reach).astype(kind)


def setup_inputs(seed: int = 0) -> dict:
    key_of = jax.random.split(jax.random.key(seed), 15)
    queries = draw_queries(jax.random.fold_in(key_of[14], 71), 0)
    new_keys = gaussian(key_of[1], (ROWS, KVH * HD), 1.0, 6.0, ((0, 32), (1, 4)))
    new_values = gaussian(key_of[2], (ROWS, KVH * HD), 1.0, 6.0, ((0, 32), (1, 4)))
    key_cache = gaussian(key_of[3], (ROWS, KVH, CAP, HD), 1.0, 6.0, ((0, 32), (1, 4)))
    value_cache = gaussian(key_of[4], (ROWS, KVH, CAP, HD), 1.0, 6.0, ((0, 32), (1, 4)))
    cache_lengths = draw_cache_lengths(jax.random.fold_in(key_of[14], 71), 0)
    out_weight = gaussian(key_of[6], (H * HD, D), (H * HD) ** -0.5, 0.0625, ((0, 4), (1, 32)))
    residual_in = gaussian(key_of[7], (ROWS, D), 1.0, 6.0, ((0, 128),))
    norm_gain = jnp.clip(1.0 + 0.15 * jax.random.normal(key_of[8], (D,), jnp.float32), 0.25, 1.75)
    expert_ids_keys = jax.random.split(jax.random.fold_in(key_of[9], 1), ROWS // ROW_SHARD)
    expert_ids_turns = jax.random.permutation(jax.random.fold_in(key_of[9], 3), ROWS // ROW_SHARD)
    expert_ids = jax.vmap(lambda own, number: routed_block(jax.random.fold_in(key_of[9], 2), own, number, ROW_SHARD, EXPERTS, TOPK, CAPY, 2))(expert_ids_keys, expert_ids_turns).reshape((ROWS, TOPK))
    route_weights = jnp.clip(jnp.exp(math.log(1.0) - 2.9957323 * jax.random.uniform(key_of[10], (ROWS, TOPK), jnp.float32) ** shard_levels(key_of[10], (ROWS, TOPK), ((0, 128),), -0.2, 0.2)), 0.05, 1.0)
    w_gate = gaussian(key_of[11], (EXPERTS, D, FFW), D ** -0.5, 0.09375, ((0, 32), (2, 4)))
    w_up = gaussian(key_of[12], (EXPERTS, D, FFW), D ** -0.5, 0.09375, ((0, 32), (2, 4)))
    w_down = gaussian(key_of[13], (EXPERTS, FFW, D), FFW ** -0.5, 0.15625, ((0, 32), (1, 4)))
    return dict(queries=queries, new_keys=new_keys, new_values=new_values, key_cache=key_cache, value_cache=value_cache, cache_lengths=cache_lengths, out_weight=out_weight, residual_in=residual_in, norm_gain=norm_gain, expert_ids=expert_ids, route_weights=route_weights, w_gate=w_gate, w_up=w_up, w_down=w_down)


def attend(queries, new_keys, new_values, key_cache, value_cache, cache_lengths):
    row_count, kv_local, slot_count, head_size = key_cache.shape
    group = queries.shape[1] // (kv_local * head_size)
    factor = 1.0 / math.sqrt(head_size)
    query = queries.reshape(row_count, kv_local, group, head_size).astype(jnp.float32)
    scores = jnp.einsum('rjgd,rjtd->rjgt', query, key_cache.astype(jnp.float32)) * factor
    fresh = jnp.einsum('rjgd,rjd->rjg', query, new_keys.reshape(row_count, kv_local, head_size).astype(jnp.float32)) * factor
    live = jnp.arange(slot_count, dtype=jnp.int32)[None, :] < cache_lengths[:, None]
    scores = jnp.where(live[:, None, None, :], scores, -1e+30)
    highest = jnp.maximum(lax.optimization_barrier(jnp.max(scores, axis=-1)), fresh)
    spread = jnp.exp(scores - highest[..., None])
    fresh_exp = jnp.exp(fresh - highest)
    denominator = lax.optimization_barrier(jnp.sum(spread, axis=-1)) + fresh_exp
    weights = (spread / denominator[..., None]).astype(jnp.bfloat16)
    fresh_weight = (fresh_exp / denominator).astype(jnp.bfloat16)
    mixed = jnp.einsum('rjgt,rjtd->rjgd', weights.astype(jnp.float32), value_cache.astype(jnp.float32))
    mixed = mixed + fresh_weight.astype(jnp.float32)[..., None] * new_values.reshape(row_count, kv_local, 1, head_size).astype(jnp.float32)
    return mixed.astype(jnp.bfloat16).reshape(row_count, kv_local * group * head_size)

def reference(queries, new_keys, new_values, key_cache, value_cache, cache_lengths, out_weight, residual_in, norm_gain, expert_ids, route_weights, w_gate, w_up, w_down):
    blocks = ROWS // ROW_DEV
    pieces = (queries.reshape(blocks, ROW_DEV, H * HD), new_keys.reshape(blocks, ROW_DEV, KVH * HD), new_values.reshape(blocks, ROW_DEV, KVH * HD), key_cache.reshape(blocks, ROW_DEV, KVH, CAP, HD), value_cache.reshape(blocks, ROW_DEV, KVH, CAP, HD), cache_lengths.reshape(blocks, ROW_DEV))

    def per_block(items):
        return attend(*items)
    attn = lax.map(per_block, pieces).reshape(ROWS, H * HD)
    proj = jnp.dot(attn, out_weight, preferred_element_type=jnp.float32)
    hidden_one = residual_in.astype(jnp.float32) + proj
    normed = (hidden_one * lax.rsqrt(lax.optimization_barrier(jnp.mean(hidden_one * hidden_one, axis=-1, keepdims=True)) + 1e-06) * norm_gain).astype(jnp.bfloat16)
    gates = route_weights / lax.optimization_barrier(jnp.sum(route_weights, axis=-1, keepdims=True))
    flat = expert_ids.reshape(-1).astype(jnp.int32)
    order = jnp.argsort(flat, stable=True).astype(jnp.int32)
    counts = lax.optimization_barrier(jnp.sum((flat[:, None] == jnp.arange(EXPERTS, dtype=jnp.int32)[None, :]).astype(jnp.int32), axis=0))
    starts = (jnp.cumsum(counts) - counts).astype(jnp.int32)
    window = ROWS // ROW_SHARD * CAPY
    padded = jnp.concatenate([order, jnp.zeros((window,), jnp.int32)])
    flat_gates = gates.reshape(-1)

    def expert_step(total, items):
        gate_mat, up_mat, down_mat, index = items
        picks = lax.dynamic_slice_in_dim(padded, starts[index], window)
        valid = jnp.arange(window, dtype=jnp.int32) < counts[index]
        source = normed[picks // TOPK]
        gate_val = jnp.dot(source, gate_mat, preferred_element_type=jnp.float32)
        up_val = jnp.dot(source, up_mat, preferred_element_type=jnp.float32)
        act = (jax.nn.silu(gate_val) * up_val).astype(jnp.bfloat16)
        result = jnp.dot(act, down_mat, preferred_element_type=jnp.float32)
        scaled = jnp.where(valid, flat_gates[picks], jnp.zeros((), jnp.float32))
        total = total.at[picks // TOPK].add(scaled[:, None] * result)
        return (total, None)
    moe_sum, _ = lax.scan(expert_step, jnp.zeros((ROWS, D), jnp.float32), (w_gate, w_up, w_down, jnp.arange(EXPERTS, dtype=jnp.int32)))
    return (hidden_one + moe_sum).astype(jnp.bfloat16)
```

```python
import math

import jax
import jax.numpy as jnp
from jax import lax
from jax.experimental import pallas as pl
from jax.experimental.pallas import tpu as pltpu
from jax.sharding import PartitionSpec as P

MESH = pl.DeviceIdType.MESH
SIDE = 4
WIDTH = 4096
BLOCK = 16
CAPACITY = 4
PARTS = (
    ("x", "y", "z", 0, 1408),
    ("y", "z", "x", 1408, 1408),
    ("z", "x", "y", 2816, 1280),
)


def my_place():
    row = lax.axis_index("dp")
    return {
        "y": row // (2 * SIDE),
        "x": (row // 2) % SIDE,
        "c": row % 2,
        "z": lax.axis_index("head"),
    }


def device_of(place):
    return ((place["y"] * SIDE + place["x"]) * 2 + place["c"], place["z"])


def shifted(place, axis, by):
    other = dict(place)
    other[axis] = (place[axis] + by) % SIDE
    return other


def sibling_of(place):
    other = dict(place)
    other["c"] = 1 - place["c"]
    return other


def greet(partners):
    barrier = pltpu.get_barrier_semaphore()
    for partner in partners:
        pl.semaphore_signal(barrier, inc=1, device_id=device_of(partner), device_id_type=MESH)
    pl.semaphore_wait(barrier, len(partners))


def remote(src, dst, send, recv, place):
    return pltpu.make_async_remote_copy(
        src_ref=src, dst_ref=dst, send_sem=send, recv_sem=recv,
        device_id=device_of(place), device_id_type=MESH,
    )


def blocks_at(ref, core, place, free, halves, columns):
    index = [core]
    last = max(free, key="zyx".index, default=None)
    for axis in ("z", "y", "x"):
        if axis in free:
            if halves is not None and axis == last:
                index.append(pl.ds(halves * (SIDE // 2), SIDE // 2))
            else:
                index.append(slice(None))
        else:
            index.append(place[axis])
    start, size = columns
    if not free and halves is not None:
        low = (size // 256) * 128
        start, size = (start, low) if halves == 0 else (start + low, size - low)
    return ref.at[(*index, slice(None), pl.ds(start, size))]


def gather_kernel(mine_ref, all_ref, own_sem, near_send, near_recv, far_send, far_recv, pair_send, pair_recv, first_send, first_recv):
    me = my_place()
    core = me["c"]
    sibling = sibling_of(me)
    greet([sibling] + [shifted(me, axis, by) for axis in "xyz" for by in (1, -1)])
    home = all_ref.at[core, me["z"], me["y"], me["x"]]
    own = pltpu.make_async_copy(mine_ref, home, own_sem)
    own.start()
    first = remote(mine_ref, home, first_send, first_recv, sibling)
    first.start()
    own.wait()
    waits = [first]

    def group(part, stage, coordinate_shift, halves=None):
        order, start, size = PARTS[part][:3], PARTS[part][3], PARTS[part][4]
        place = shifted(me, order[stage], coordinate_shift)
        return blocks_at(all_ref, core, place, order[:stage], halves, (start, size))

    def to_pair(part, stage, number, block):
        copy = remote(block, block, pair_send.at[part, stage, number], pair_recv.at[part, stage, number], sibling)
        copy.start()
        waits.append(copy)

    for stage in range(3):
        near = {}
        for part in range(3):
            axis = PARTS[part][stage]
            block = group(part, stage, 0)
            for way, by in ((0, 1), (1, -1)):
                copy = remote(block, block, near_send.at[part, stage, way], near_recv.at[part, stage, way], shifted(me, axis, by))
                copy.start()
                near[part, way] = copy
        far = {}
        for part in range(3):
            axis = PARTS[part][stage]
            for way, by in ((0, 1), (1, -1)):
                near[part, way].wait_recv()
                block = group(part, stage, -by, way)
                copy = remote(block, block, far_send.at[part, stage, way], far_recv.at[part, stage, way], shifted(me, axis, by))
                copy.start()
                far[part, way] = copy
                to_pair(part, stage, way, group(part, stage, -by))
        for part in range(3):
            for way in (0, 1):
                far[part, way].wait_recv()
            to_pair(part, stage, 2, group(part, stage, 2))
        for part in range(3):
            for way in (0, 1):
                near[part, way].wait_send()
                far[part, way].wait_send()
    for copy in waits:
        copy.wait()


def gather_rows(mine):
    return pl.pallas_call(
        gather_kernel,
        out_shape=jax.ShapeDtypeStruct((2, SIDE, SIDE, SIDE, BLOCK, WIDTH), jnp.bfloat16),
        in_specs=[pl.BlockSpec(memory_space=pl.ANY)],
        out_specs=pl.BlockSpec(memory_space=pl.ANY),
        scratch_shapes=[
            pltpu.SemaphoreType.DMA,
            pltpu.SemaphoreType.DMA((3, 3, 2)),
            pltpu.SemaphoreType.DMA((3, 3, 2)),
            pltpu.SemaphoreType.DMA((3, 3, 2)),
            pltpu.SemaphoreType.DMA((3, 3, 2)),
            pltpu.SemaphoreType.DMA((3, 3, 3)),
            pltpu.SemaphoreType.DMA((3, 3, 3)),
            pltpu.SemaphoreType.DMA,
            pltpu.SemaphoreType.DMA,
        ],
        compiler_params=pltpu.CompilerParams(collective_id=1, has_side_effects=True),
    )(mine)


def reduce_kernel(parts_ref, base_ref, out_ref, acc, pair_buf, near1, near2, near3, far1, far2, far3,
                  local_sem, pair_send, pair_recv, near_send, near_recv, far_send, far_recv):
    me = my_place()
    core = me["c"]
    sibling = sibling_of(me)
    near_bufs, far_bufs = (near1, near2, near3), (far1, far2, far3)
    greet([sibling] + [shifted(me, axis, by) for axis in "xyz" for by in (1, -1)])
    waits = []

    def axis_of(part, stage):
        return PARTS[part][2 - stage]

    def free_of(part, stage):
        return PARTS[part][: 2 - stage]

    def columns_of(part):
        return PARTS[part][3], PARTS[part][4]

    def group(ref, part, stage, shift, which, halves=None):
        place = shifted(me, axis_of(part, stage), shift)
        return blocks_at(ref, which, place, free_of(part, stage), halves, columns_of(part))

    shifts = (2, 1, -1, 0)
    pair, local = {}, {}
    for number, shift in enumerate(shifts):
        for part in range(3):
            copy = remote(
                group(parts_ref, part, 0, shift, 1 - core),
                group(pair_buf, part, 0, shift, 0),
                pair_send.at[part, number], pair_recv.at[part, number], sibling,
            )
            copy.start()
            pair[part, number] = copy
            waits.append(copy)
            copy = pltpu.make_async_copy(group(parts_ref, part, 0, shift, core), group(acc, part, 0, shift, 0), local_sem.at[part, number])
            copy.start()
            local[part, number] = copy

    def add_into(target, others):
        lead = target.shape[:-2]
        count = 1
        for size in lead:
            count *= size

        def body(at, _):
            index = []
            rest = at
            for size in reversed(lead):
                index.insert(0, rest % size)
                rest = rest // size
            index = (*index, slice(None), slice(None))
            total = target[index].astype(jnp.float32)
            for other in others:
                total += other[index].astype(jnp.float32)
            target[index] = total.astype(target.dtype)
            return 0

        if count == 1:
            body(0, 0)
        else:
            lax.fori_loop(0, count, body, 0)

    for stage in range(3):
        near, far = {}, {}

        def far_copy(part, way):
            axis = axis_of(part, stage)
            by = 1 if way == 0 else -1
            src = group(acc, part, stage, 2, 0, way)
            dst = far_bufs[stage].at[part, way, ..., pl.ds(0, src.shape[-1])]
            return remote(src, dst,
                          far_send.at[part, stage, way], far_recv.at[part, stage, way], shifted(me, axis, by))

        def near_copy(part, way, half):
            axis = axis_of(part, stage)
            by = 1 if way == 0 else -1
            src = group(acc, part, stage, by, 0, half)
            dst = near_bufs[stage].at[part, way, half, ..., pl.ds(0, src.shape[-1])]
            return remote(src, dst, near_send.at[part, stage, way, half], near_recv.at[part, stage, way, half], shifted(me, axis, by))

        for part in range(3):
            if stage == 0:
                local[part, 0].wait()
                pair[part, 0].wait_recv()
                add_into(group(acc, part, 0, 2, 0), [group(pair_buf, part, 0, 2, 0)])
            for way in (0, 1):
                far[part, way] = far_copy(part, way)
                far[part, way].start()
        for part in range(3):
            for way, by in ((0, 1), (1, -1)):
                if stage == 0:
                    local[part, 1 + way].wait()
                    pair[part, 1 + way].wait_recv()
                    add_into(group(acc, part, 0, by, 0), [group(pair_buf, part, 0, by, 0)])
                near[part, way, 1 - way] = near_copy(part, way, 1 - way)
                near[part, way, 1 - way].start()
        for part in range(3):
            for way, by in ((0, 1), (1, -1)):
                far[part, way].wait_recv()
                target = group(acc, part, stage, by, 0, way)
                add_into(target, [far_bufs[stage].at[part, way, ..., pl.ds(0, target.shape[-1])]])
                near[part, way, way] = near_copy(part, way, way)
                near[part, way, way].start()
        for part in range(3):
            if stage == 0:
                local[part, 3].wait()
                pair[part, 3].wait_recv()
                add_into(group(acc, part, 0, 0, 0), [group(pair_buf, part, 0, 0, 0)])
        for part in range(3):
            for half in (0, 1):
                for way in (0, 1):
                    near[part, way, half].wait_recv()
                target = group(acc, part, stage, 0, 0, half)
                others = [near_bufs[stage].at[part, way, half, ..., pl.ds(0, target.shape[-1])] for way in (0, 1)]
                if stage < 2:
                    add_into(target, others)
                else:
                    total = target[...].astype(jnp.float32)
                    for other in others:
                        total += other[...].astype(jnp.float32)
                    start, size = columns_of(part)
                    low = (size // 256) * 128
                    start, size = (start, low) if half == 0 else (start + low, size - low)
                    out_ref[:, pl.ds(start, size)] = (base_ref[:, pl.ds(start, size)] + total).astype(out_ref.dtype)
        for copy in [*near.values(), *far.values()]:
            copy.wait_send()
    for copy in waits:
        copy.wait_send()


def reduce_rows(parts, base):
    wide = 1408
    half = SIDE // 2
    vmem = pl.BlockSpec(memory_space=pltpu.VMEM)
    return pl.pallas_call(
        reduce_kernel,
        out_shape=jax.ShapeDtypeStruct((BLOCK, WIDTH), jnp.bfloat16),
        in_specs=[pl.BlockSpec(memory_space=pl.ANY), vmem],
        out_specs=vmem,
        scratch_shapes=[
            pltpu.VMEM((1, SIDE, SIDE, SIDE, BLOCK, WIDTH), jnp.bfloat16),
            pltpu.VMEM((1, SIDE, SIDE, SIDE, BLOCK, WIDTH), jnp.bfloat16),
            pltpu.VMEM((3, 2, 2, SIDE, half, BLOCK, wide), jnp.bfloat16),
            pltpu.VMEM((3, 2, 2, half, BLOCK, wide), jnp.bfloat16),
            pltpu.VMEM((3, 2, 2, BLOCK, wide // 2 + 64), jnp.bfloat16),
            pltpu.VMEM((3, 2, SIDE, half, BLOCK, wide), jnp.bfloat16),
            pltpu.VMEM((3, 2, half, BLOCK, wide), jnp.bfloat16),
            pltpu.VMEM((3, 2, BLOCK, wide // 2 + 64), jnp.bfloat16),
            pltpu.SemaphoreType.DMA((3, 4)),
            pltpu.SemaphoreType.DMA((3, 4)),
            pltpu.SemaphoreType.DMA((3, 4)),
            pltpu.SemaphoreType.DMA((3, 3, 2, 2)),
            pltpu.SemaphoreType.DMA((3, 3, 2, 2)),
            pltpu.SemaphoreType.DMA((3, 3, 2)),
            pltpu.SemaphoreType.DMA((3, 3, 2)),
        ],
        compiler_params=pltpu.CompilerParams(collective_id=2, has_side_effects=True, vmem_limit_bytes=60 * 1024 * 1024),
    )(parts, base)


def attend(queries, new_keys, new_values, key_cache, value_cache, cache_lengths):
    row_count, kv_local, slot_count, head_size = key_cache.shape
    group = queries.shape[1] // (kv_local * head_size)
    factor = 1.0 / math.sqrt(head_size)
    block = math.gcd(128, slot_count)
    used = (jnp.max(cache_lengths) + block - 1) // block
    query = queries.reshape(row_count, kv_local, group, head_size)
    fresh = (
        jnp.einsum(
            "rjgd,rjd->rjg",
            query,
            new_keys.reshape(row_count, kv_local, head_size),
            preferred_element_type=jnp.float32,
        )
        * factor
    )

    def score_block(index, buffer):
        start = index * block
        keys = lax.dynamic_slice_in_dim(key_cache, start, block, 2)
        part_scores = (
            jnp.einsum("rjgd,rjtd->rjgt", query, keys, preferred_element_type=jnp.float32) * factor
        )
        return lax.dynamic_update_slice_in_dim(buffer, part_scores, start, 3)

    scores = lax.fori_loop(
        0, used, score_block, jnp.full((row_count, kv_local, group, slot_count), -1e30, jnp.float32)
    )
    live = jnp.arange(slot_count, dtype=jnp.int32)[None, :] < cache_lengths[:, None]
    scores = jnp.where(live[:, None, None, :], scores, -1e30)
    highest = jnp.maximum(jnp.max(scores, axis=-1), fresh)
    spread = jnp.exp(scores - highest[..., None])
    fresh_exp = jnp.exp(fresh - highest)
    denominator = jnp.sum(spread, axis=-1) + fresh_exp
    weights = (spread / denominator[..., None]).astype(jnp.bfloat16)
    fresh_weight = (fresh_exp / denominator).astype(jnp.bfloat16)

    def mix_block(index, total):
        start = index * block
        weight_part = lax.dynamic_slice_in_dim(weights, start, block, 3)
        values = lax.dynamic_slice_in_dim(value_cache, start, block, 2)
        return total + jnp.einsum(
            "rjgt,rjtd->rjgd", weight_part, values, preferred_element_type=jnp.float32
        )

    mixed = lax.fori_loop(
        0, used, mix_block, jnp.zeros((row_count, kv_local, group, head_size), jnp.float32)
    )
    mixed = mixed + fresh_weight.astype(jnp.float32)[..., None] * new_values.reshape(
        row_count, kv_local, 1, head_size
    ).astype(jnp.float32)
    return mixed.astype(jnp.bfloat16).reshape(row_count, kv_local * group * head_size)


def route_codes(expert_ids, route_weights):
    gates = route_weights / jnp.sum(route_weights, axis=-1, keepdims=True)
    rows = expert_ids.shape[0]
    same = jnp.any(expert_ids[:, :, None, None] == expert_ids[None, None, :, :], axis=-1)
    earlier = jnp.arange(rows)[None, None, :] < jnp.arange(rows)[:, None, None]
    position = jnp.sum((same & earlier).astype(jnp.int32), axis=-1)
    codes = (expert_ids * CAPACITY + position).astype(jnp.float32)
    return jnp.stack([codes.T.reshape(-1), gates.T.reshape(-1)])


def experts(rows, codes, w_gate, w_up, w_down):
    groups, span = 8, 256
    tokens = rows.reshape(groups, span, WIDTH)
    choices = codes.shape[-1] // BLOCK
    table = codes.reshape(SIDE, SIDE, 2, SIDE, 2, choices, BLOCK)
    table = table.transpose(4, 5, 2, 3, 0, 1, 6).reshape(2, choices, groups, span // BLOCK, BLOCK)
    first = (lax.axis_index("dp") * 2 * CAPACITY).astype(jnp.float32)
    place = jnp.arange(span // BLOCK, dtype=jnp.float32)[None, :, None] * CAPACITY
    slots, weights = [], []
    for own in range(2):
        code = table[0] - (first + own * CAPACITY)
        hit = (code >= 0) & (code < CAPACITY)
        slot = jnp.sum(jnp.where(hit, code + 1, 0.0), axis=0)
        slots.append(jnp.where(slot > 0, slot - 1 + place + own * 64, -1.0).reshape(groups, span))
        weights.append(jnp.sum(jnp.where(hit, table[1], 0.0), axis=0).reshape(groups, span))
    spot = jnp.arange(128, dtype=jnp.float32)[None, :, None]
    picks = [spot == slot[:, None, :] for slot in slots]
    pick = (picks[0] | picks[1]).astype(jnp.bfloat16)
    scale = jnp.sum(jnp.where(picks[0], weights[0][:, None, :], 0.0) + jnp.where(picks[1], weights[1][:, None, :], 0.0), axis=-1)
    chosen = jnp.einsum("gsr,grd->gsd", pick, tokens, preferred_element_type=jnp.float32).astype(jnp.bfloat16)
    chosen = chosen.reshape(groups, 2, 64, WIDTH)
    scale = scale.reshape(groups, 2, 64)
    gate_val = jnp.einsum("gesd,edf->gesf", chosen, w_gate, preferred_element_type=jnp.float32)
    up_val = jnp.einsum("gesd,edf->gesf", chosen, w_up, preferred_element_type=jnp.float32)
    act = (jax.nn.silu(gate_val) * up_val * scale[..., None]).astype(jnp.bfloat16)
    result = jnp.einsum("gesf,efd->gesd", act, w_down, preferred_element_type=jnp.float32).astype(jnp.bfloat16)
    result = result.reshape(groups, 128, WIDTH)
    spread = jnp.einsum("gsr,gsd->grd", pick, result, preferred_element_type=jnp.float32).astype(jnp.bfloat16)
    return spread.reshape(2, SIDE, SIDE, SIDE, BLOCK, WIDTH)


def on_device(
    queries,
    new_keys,
    new_values,
    key_cache,
    value_cache,
    cache_lengths,
    out_weight,
    residual_in,
    norm_gain,
    expert_ids,
    route_weights,
    w_gate,
    w_up,
    w_down,
):
    dp_count = lax.axis_size("dp")
    head_count = lax.axis_size("head")
    codes = lax.all_gather(route_codes(expert_ids, route_weights), ("dp", "head"), axis=0, tiled=False)
    attn = attend(queries, new_keys, new_values, key_cache, value_cache, cache_lengths)
    group_rows = attn.shape[0]
    feature_cols = out_weight.shape[1]
    share_rows = group_rows // head_count
    width = residual_in.shape[1]
    partial_proj = jnp.dot(
        lax.all_gather(attn, "dp", axis=0, tiled=True),
        out_weight,
        preferred_element_type=jnp.float32,
    )
    ordered = partial_proj.reshape(dp_count, head_count, share_rows, feature_cols).transpose(
        1, 0, 2, 3
    )
    ordered = ordered.reshape(head_count * dp_count * share_rows, feature_cols)
    summed_proj = lax.psum(ordered, "head")
    mine = lax.dynamic_slice_in_dim(
        summed_proj, lax.axis_index("head") * dp_count * share_rows, dp_count * share_rows, 0
    )
    proj = lax.all_to_all(mine, "dp", split_axis=0, concat_axis=1, tiled=True)
    hidden_one = residual_in.astype(jnp.float32) + proj
    normed = (
        hidden_one
        * lax.rsqrt(jnp.mean(hidden_one * hidden_one, axis=-1, keepdims=True) + 1e-06)
        * norm_gain
    ).astype(jnp.bfloat16)
    rows = gather_rows(normed)
    partial_out = experts(rows, codes, w_gate, w_up, w_down)
    return reduce_rows(partial_out, hidden_one)


def solution(mesh):
    in_specs = (
        P("dp", "head"),
        P("dp", "head"),
        P("dp", "head"),
        P("dp", "head", None, None),
        P("dp", "head", None, None),
        P("dp"),
        P("head", "dp"),
        P(("dp", "head"), None),
        P(),
        P(("dp", "head"), None),
        P(("dp", "head"), None),
        P("dp", None, "head"),
        P("dp", None, "head"),
        P("dp", "head", None),
    )
    out_specs = P(("dp", "head"), None)
    return jax.shard_map(
        on_device, mesh=mesh, in_specs=in_specs, out_specs=out_specs, check_vma=False
    )
```

```python
import math

import jax
import jax.numpy as jnp
from jax import lax
from jax.experimental import pallas as pl
from jax.experimental.pallas import tpu as pltpu
from jax.sharding import PartitionSpec as P

MESH = pl.DeviceIdType.MESH
SIDE = 4
WIDTH = 4096
BLOCK = 16
CAPACITY = 4
CHOICES = 8
SLOTS = 64
ORDERS = (("x", "y", "z"), ("y", "z", "x"), ("z", "x", "y"))
WAVES = 2
PARTS = ORDERS * WAVES
WIDE = WIDTH + 256
TILES_OUT = (6, 6, 5)
TILES_BACK = (6, 6, 6, 5, 5, 4)
DIRECT_OUT = ((0, 0), (0, 1))
DIRECT_BACK = ((1, 1), (1, 2))
WIDEST = 768


def columns_of(tiles, part):
    return 128 * sum(tiles[:part]), 128 * tiles[part]


def my_place():
    row = lax.axis_index("dp")
    return {
        "y": row // (2 * SIDE),
        "x": (row // 2) % SIDE,
        "c": row % 2,
        "z": lax.axis_index("head"),
    }


def device_of(place):
    return ((place["y"] * SIDE + place["x"]) * 2 + place["c"], place["z"])


def shifted(place, axis, by):
    other = dict(place)
    other[axis] = (place[axis] + by) % SIDE
    return other


def sibling_of(place):
    other = dict(place)
    other["c"] = 1 - place["c"]
    return other


def greet(partners):
    barrier = pltpu.get_barrier_semaphore()
    for partner in partners:
        pl.semaphore_signal(barrier, inc=1, device_id=device_of(partner), device_id_type=MESH)
    pl.semaphore_wait(barrier, len(partners))


def remote(src, dst, send, recv, place):
    return pltpu.make_async_remote_copy(
        src_ref=src, dst_ref=dst, send_sem=send, recv_sem=recv,
        device_id=device_of(place), device_id_type=MESH,
    )


def blocks_at(ref, core, place, free, halves, columns):
    index = [core]
    last = max(free, key="zyx".index, default=None)
    for axis in ("z", "y", "x"):
        if axis in free:
            if halves is not None and axis == last:
                index.append(pl.ds(halves * (SIDE // 2), SIDE // 2))
            else:
                index.append(slice(None))
        else:
            index.append(place[axis])
    start, size = columns
    if not free and halves is not None:
        low = (size // 256) * 128
        start, size = (start, low) if halves == 0 else (start + low, size - low)
    return ref.at[(*index, slice(None), pl.ds(start, size))]


def attend_rows(base, rows, lengths_ref, query_ref, fresh_key_ref, fresh_value_ref, keys, values, attn_ref):
    slots, head_size = keys.shape[1:]
    heads = query_ref.shape[1] // head_size
    factor = 1.0 / math.sqrt(head_size)
    slot = lax.broadcasted_iota(jnp.int32, (heads, slots), 1)
    block = pl.ds(base, rows)
    query = jnp.stack([query_ref[block, head * head_size : (head + 1) * head_size].astype(jnp.float32) for head in range(heads)])
    query = jnp.swapaxes(query, 0, 1)
    narrow = query.astype(jnp.bfloat16)
    scores = []
    for row in range(rows):
        score = lax.dot_general(narrow[row], keys[base + row], (((1,), (1,)), ((), ())), preferred_element_type=jnp.float32)
        scores.append(jnp.where(slot < lengths_ref[base + row], score * factor, -1e30))
    scores = jnp.concatenate(scores, axis=0)
    fresh_key = fresh_key_ref[block].astype(jnp.float32).reshape(rows, 1, head_size)
    fresh = jnp.sum(query * fresh_key, axis=-1, keepdims=True).reshape(rows * heads, 1) * factor
    highest = jnp.maximum(jnp.max(scores, axis=-1, keepdims=True), fresh)
    spread = jnp.exp(scores - highest)
    fresh_exp = jnp.exp(fresh - highest)
    inverse = 1.0 / (jnp.sum(spread, axis=-1, keepdims=True) + fresh_exp)
    weights = (spread * inverse).astype(jnp.bfloat16)
    fresh_weight = (fresh_exp * inverse).astype(jnp.bfloat16).astype(jnp.float32)
    mixed = [
        jnp.dot(weights[row * heads : (row + 1) * heads], values[base + row], preferred_element_type=jnp.float32)
        for row in range(rows)
    ]
    fresh_value = fresh_value_ref[block].astype(jnp.float32).reshape(rows, 1, head_size)
    mixed = jnp.concatenate(mixed, axis=0).reshape(rows, heads, head_size) + fresh_weight.reshape(rows, heads, 1) * fresh_value
    mixed = jnp.swapaxes(mixed, 0, 1).astype(jnp.bfloat16)
    for head in range(heads):
        attn_ref[block, head * head_size : (head + 1) * head_size] = mixed[head]


def route_block(names_ref, names, weights, table):
    choices, rows = names.shape
    lane = lax.broadcasted_iota(jnp.int32, (choices, rows), 1)
    position = jnp.zeros((choices, rows), jnp.int32)
    for row in range(rows):
        same = names == names_ref[0, row]
        for choice in range(1, choices):
            same = same | (names == names_ref[choice, row])
        position += jnp.where(same & (lane > row), 1, 0)
    gates = weights / jnp.sum(weights, axis=0, keepdims=True)
    upper = gates.astype(jnp.bfloat16).astype(jnp.float32)
    table[...] = jnp.zeros_like(table)
    table[0:choices, 0:rows] = (names * CAPACITY + position).astype(jnp.float32)
    table[choices : 2 * choices, 0:rows] = upper
    table[2 * choices : 3 * choices, 0:rows] = gates - upper
    return table[...].T[0:rows].astype(jnp.bfloat16)


def attend_and_project_kernel(lengths_ref, names_ref, query_in, fresh_key_in, fresh_value_in, key_ref, value_ref,
                              weight_ref, residual_in, gain_in, names_in, weights_in, hidden_ref, normed_ref,
                              query_ref, fresh_key_ref, fresh_value_ref, residual_ref, gain_ref, names_here, weights_here, table,
                              attn_ref, keys, values, attn_all, weight_all, sums, sums_in, mine, mine_in,
                   local_sem, input_sem, key_sem, value_sem, w_send, w_recv, a_send, a_recv, p_send, p_recv, s_send, s_recv, m_send, m_recv):
    me = my_place()
    sibling = sibling_of(me)
    rows, depth = attn_ref.shape
    inputs = [
        pltpu.make_async_copy(src, dst, input_sem.at[at])
        for at, (src, dst) in enumerate((
            (query_in, query_ref), (fresh_key_in, fresh_key_ref), (fresh_value_in, fresh_value_ref), (residual_in, residual_ref),
            (gain_in, gain_ref), (names_in, names_here), (weights_in, weights_here),
        ))
    ]
    for load in inputs:
        load.start()
    own_cols = weight_ref.shape[1]
    half_depth, half_rows = depth // 2, rows // 2
    step = 16
    loads = []
    for at in range(rows // step):
        block = pl.ds(at * step, step)
        loads.append((pltpu.make_async_copy(key_ref.at[block, 0], keys.at[block], key_sem.at[at]),
                      pltpu.make_async_copy(value_ref.at[block, 0], values.at[block], value_sem.at[at])))
        for load in loads[-1]:
            load.start()

    def neighbour(by, core):
        other = shifted(me, "x", by)
        other["c"] = (me["c"] + core) % 2
        return other

    others = [(by, core) for by in range(SIDE) for core in range(2) if by or core]
    greet([neighbour(*which) for which in others] + [shifted(me, axis, by) for axis in "yz" for by in (1, 2, 3)])

    def weight_at(by, low=0, size=depth):
        column = ((me["y"] + by) % SIDE) * own_cols
        return weight_all.at[pl.ds(low, size), pl.ds(pl.multiple_of(column, own_cols), own_cols)]

    def attn_at(by, core, low=0, size=rows):
        return attn_all.at[(me["x"] + by) % SIDE, core, pl.ds(low, size)]

    core = me["c"]
    own_w = pltpu.make_async_copy(weight_ref, weight_at(0), local_sem.at[0])
    own_w.start()
    started = []

    def go(src, dst, send, recv, place):
        copy = remote(src, dst, send, recv, place)
        copy.start()
        started.append(copy)
        return copy

    near_w, near_a, far_w, far_a, pair = {}, {}, {}, {}, {}
    for way, by in ((0, 1), (1, -1)):
        near_w[way] = go(weight_ref, weight_at(0), w_send.at[way], w_recv.at[way], shifted(me, "y", by))
    for load in inputs:
        load.wait()
    for at in range(rows // step):
        for load in loads[at]:
            load.wait()
        attend_rows(at * step, step, lengths_ref, query_ref, fresh_key_ref, fresh_value_ref, keys, values, attn_ref)
    own_a = pltpu.make_async_copy(attn_ref, attn_at(0, core), local_sem.at[1])
    own_a.start()
    for way, by in ((0, 1), (1, -1)):
        near_a[way] = go(attn_ref, attn_at(0, core), a_send.at[way], a_recv.at[way], shifted(me, "x", by))
    pair[0] = go(attn_ref, attn_at(0, core), p_send.at[0], p_recv.at[0], sibling)
    for way, by in ((0, 1), (1, -1)):
        near_w[way].wait_recv()
        block = weight_at(-by, way * half_depth, half_depth)
        far_w[way] = go(block, block, w_send.at[2 + way], w_recv.at[2 + way], shifted(me, "y", by))
    for way, by in ((0, 1), (1, -1)):
        near_a[way].wait_recv()
        block = attn_at(-by, core, way * half_rows, half_rows)
        far_a[way] = go(block, block, a_send.at[2 + way], a_recv.at[2 + way], shifted(me, "x", by))
        block = attn_at(-by, core)
        pair[-by] = go(block, block, p_send.at[1 + way], p_recv.at[1 + way], sibling)
    for way in (0, 1):
        far_a[way].wait_recv()
    block = attn_at(2, core)
    pair[2] = go(block, block, p_send.at[3], p_recv.at[3], sibling)
    normed_ref[:, WIDTH : WIDTH + 128] = route_block(names_ref, names_here[...], weights_here[...], table)
    normed_ref[:, WIDTH + 128 :] = jnp.zeros((rows // SIDE, WIDE - WIDTH - 128), normed_ref.dtype)
    own_w.wait()
    own_a.wait()
    for way in (0, 1):
        far_w[way].wait_recv()

    share = rows // SIDE
    width = weight_all.shape[1]
    order = (0, 1, -1, 2)
    to_head = {}
    for number, by in enumerate(order):
        pair[by].wait_recv()
        at = (me["x"] + by) % SIDE
        block = attn_all[at].reshape(2 * rows, depth)
        part = jnp.dot(block, weight_all[...], preferred_element_type=jnp.float32).astype(jnp.bfloat16)
        part = part.reshape(2, SIDE, share, width)
        for head in range(SIDE):
            sums[head, at] = part[:, head]
        for away in (1, 2, 3):
            target = shifted(me, "z", away)
            to_head[number, away] = go(sums.at[target["z"], at], sums_in.at[away - 1, at],
                                       s_send.at[number, away - 1], s_recv.at[number, away - 1], target)
    slots = {}
    for number, by in enumerate(order):
        at = (me["x"] + by) % SIDE
        for away in (1, 2, 3):
            to_head[number, away].wait_recv()
        total = sums[me["z"], at].astype(jnp.float32)
        for away in range(3):
            total += sums_in[away, at].astype(jnp.float32)
        mine[number] = total.astype(jnp.bfloat16)
        for flip in (0, 1):
            if by == 0 and flip == 0:
                continue
            target = neighbour(by, flip)
            slots[number, flip] = go(mine.at[number, target["c"]], mine_in.at[me["x"], core],
                                     m_send.at[number, flip], m_recv.at[number, flip], target)
    keep = pltpu.make_async_copy(mine.at[0, core], mine_in.at[me["x"], core], local_sem.at[2])
    keep.start()
    keep.wait()
    for copy in slots.values():
        copy.wait_recv()
    square = jnp.zeros((share, 1), jnp.float32)
    for y in range(SIDE):
        for x in range(SIDE):
            for c in range(2):
                start = ((y * SIDE + x) * 2 + c) * own_cols
                value = residual_ref[:, start : start + own_cols].astype(jnp.float32)
                value += mine_in[x, c, :, y * own_cols : (y + 1) * own_cols].astype(jnp.float32)
                hidden_ref[:, start : start + own_cols] = value
                square += jnp.sum(value * value, axis=-1, keepdims=True)
    scale = lax.rsqrt(square / WIDTH + 1e-06)
    for start in range(0, WIDTH, 512):
        normed_ref[:, start : start + 512] = (hidden_ref[:, start : start + 512] * scale * gain_ref[:, start : start + 512]).astype(jnp.bfloat16)
    for copy in started:
        copy.wait_send()


def attend_and_project(queries, new_keys, new_values, key_cache, value_cache, cache_lengths, out_weight, residual, gain, expert_ids, route_weights):
    rows, _, slots, head_size = key_cache.shape
    depth = queries.shape[1]
    own_cols = out_weight.shape[1]
    width = SIDE * own_cols
    share = rows // SIDE
    vmem, hbm, smem = (pl.BlockSpec(memory_space=space) for space in (pltpu.VMEM, pl.ANY, pltpu.SMEM))
    names, route_weights = expert_ids.T, route_weights.T
    bf16 = jnp.bfloat16
    dma = pltpu.SemaphoreType.DMA
    return pl.pallas_call(
        attend_and_project_kernel,
        out_shape=(
            jax.ShapeDtypeStruct((share, WIDTH), jnp.float32),
            jax.ShapeDtypeStruct((share, WIDE), bf16),
        ),
        in_specs=[smem, smem] + [hbm] * 10,
        out_specs=(vmem, vmem),
        scratch_shapes=[
            pltpu.VMEM((rows, depth), bf16),
            pltpu.VMEM(new_keys.shape, bf16),
            pltpu.VMEM(new_values.shape, bf16),
            pltpu.VMEM(residual.shape, bf16),
            pltpu.VMEM((1, WIDTH), jnp.float32),
            pltpu.VMEM(names.shape, jnp.int32),
            pltpu.VMEM(names.shape, jnp.float32),
            pltpu.VMEM((128, 128), jnp.float32),
            pltpu.VMEM((rows, depth), bf16),
            pltpu.VMEM((rows, slots, head_size), bf16),
            pltpu.VMEM((rows, slots, head_size), bf16),
            pltpu.VMEM((SIDE, 2, rows, depth), bf16),
            pltpu.VMEM((depth, width), bf16),
            pltpu.VMEM((SIDE, SIDE, 2, share, width), bf16),
            pltpu.VMEM((SIDE - 1, SIDE, 2, share, width), bf16),
            pltpu.VMEM((SIDE, 2, share, width), bf16),
            pltpu.VMEM((SIDE, 2, share, width), bf16),
            dma((3,)), dma((7,)), dma((rows // 16,)), dma((rows // 16,)),
            dma((4,)), dma((4,)), dma((4,)), dma((4,)), dma((4,)), dma((4,)),
            dma((4, 3)), dma((4, 3)), dma((4, 2)), dma((4, 2)),
        ],
        compiler_params=pltpu.CompilerParams(collective_id=3, has_side_effects=True, vmem_limit_bytes=60 * 1024 * 1024),
    )(cache_lengths, names, queries, new_keys, new_values, key_cache, value_cache, out_weight, residual, gain.reshape(1, WIDTH), names, route_weights)


def pick_group(table):
    span = table.shape[0]
    lane = lax.broadcasted_iota(jnp.int32, table.shape, 1)
    row = lax.broadcasted_iota(jnp.int32, (span, 1), 0)
    place = (row // BLOCK * CAPACITY).astype(jnp.float32)
    first = (lax.axis_index("dp") * 2 * CAPACITY).astype(jnp.float32)
    spot = lane.astype(jnp.float32)
    picked = jnp.zeros(table.shape, jnp.float32)
    gates = jnp.zeros(table.shape, jnp.float32)
    for own in range(2):
        code = table - (first + own * CAPACITY)
        hit = jnp.where((lane < CHOICES) & (code >= 0) & (code < CAPACITY), 1.0, 0.0)
        slot = jnp.sum(hit * (code + 1), axis=-1, keepdims=True)
        slot = jnp.where(slot > 0, slot - 1 + place + own * SLOTS, -1.0)
        gate = jnp.sum(table * (pltpu.roll(hit, CHOICES, 1) + pltpu.roll(hit, 2 * CHOICES, 1)), axis=-1, keepdims=True)
        match = spot == slot
        picked += jnp.where(match, 1.0, 0.0)
        gates += jnp.where(match, gate, 0.0)
    scale = jnp.broadcast_to(jnp.sum(gates, axis=0, keepdims=True), (128, 128)).T
    return picked, scale


def open_kernel(mine_ref, gate_ref, up_ref, act_ref, pick_ref, everyone, gate_w, up_w, chosen, scales, gate_sum, up_sum,
                own_sem, weight_sem, near_send, near_recv, far_send, far_recv, pair_send, pair_recv, first_send, first_recv):
    me = my_place()
    core = me["c"]
    sibling = sibling_of(me)
    loads = [pltpu.make_async_copy(gate_ref, gate_w, weight_sem.at[0]), pltpu.make_async_copy(up_ref, up_w, weight_sem.at[1])]
    greet([sibling] + [shifted(me, axis, by) for axis in "xyz" for by in (1, 2, 3)])
    home = everyone.at[core, me["z"], me["y"], me["x"]]
    own = pltpu.make_async_copy(mine_ref, home, own_sem)
    own.start()
    first = remote(mine_ref, home, first_send, first_recv, sibling)
    first.start()
    own.wait()
    first.wait_recv()
    near, far, pair = {}, {}, {}

    def group(part, stage, coordinate_shift, halves=None):
        order = PARTS[part]
        place = shifted(me, order[stage], coordinate_shift)
        start, size = columns_of(TILES_OUT, part % 3)
        start = pl.multiple_of(core * (WIDE // 2) + start, 128)
        return blocks_at(everyone, part // 3, place, order[:stage], halves, (start, size))

    def to_pair(part, stage, number, block):
        copy = remote(block, block, pair_send.at[part, stage, number], pair_recv.at[part, stage, number], sibling)
        copy.start()
        pair[part, stage, number] = copy

    def send_near(wave, stage):
        for part in range(3 * wave, 3 * wave + 3):
            block = group(part, stage, 0)
            if (wave, stage) in DIRECT_OUT:
                copy = remote(block, block, far_send.at[part, stage, 0], far_recv.at[part, stage, 0], shifted(me, PARTS[part][stage], 2))
                copy.start()
                far[part, stage, 0] = copy
            for way, by in ((0, 1), (1, -1)):
                copy = remote(block, block, near_send.at[part, stage, way], near_recv.at[part, stage, way], shifted(me, PARTS[part][stage], by))
                copy.start()
                near[part, stage, way] = copy

    def send_far(wave, stage):
        for part in range(3 * wave, 3 * wave + 3):
            for way, by in ((0, 1), (1, -1)):
                near[part, stage, way].wait_recv()
                if (wave, stage) not in DIRECT_OUT:
                    block = group(part, stage, -by, way)
                    copy = remote(block, block, far_send.at[part, stage, way], far_recv.at[part, stage, way], shifted(me, PARTS[part][stage], by))
                    copy.start()
                    far[part, stage, way] = copy
                to_pair(part, stage, way, group(part, stage, -by))

    def take_far(wave, stage):
        for part in range(3 * wave, 3 * wave + 3):
            for way in (0, 1):
                if (part, stage, way) in far:
                    far[part, stage, way].wait_recv()
            to_pair(part, stage, 2, group(part, stage, 2))

    groups, span = pick_ref.shape[0], pick_ref.shape[1]

    def choose(at, _):
        c, z = at // SIDE, at % SIDE
        picked, scale = pick_group(everyone[c, z, :, :, :, WIDTH : WIDTH + 128].reshape(span, 128).astype(jnp.float32))
        pick_ref[at] = picked.astype(jnp.bfloat16)
        turned = picked.T.astype(jnp.bfloat16)
        for half in range(2):
            scales[half, at] = scale[half * SLOTS : half * SLOTS + SLOTS]
        for start in range(0, WIDTH, 512):
            rows = everyone[c, z, :, :, :, start : start + 512].reshape(span, 512)
            part = jnp.dot(turned, rows, preferred_element_type=jnp.float32).astype(jnp.bfloat16)
            for half in range(2):
                chosen[half, at, :, start : start + 512] = part[half * SLOTS : half * SLOTS + SLOTS]
        return 0

    depth = 1024
    share = groups // 2

    def open_one(wave, own):
        gate_sum[...] = jnp.zeros_like(gate_sum)
        up_sum[...] = jnp.zeros_like(up_sum)

        def multiply(step, _):
            columns = pl.ds(pl.multiple_of(step * depth, depth), depth)
            rows = chosen[own, wave * share : (wave + 1) * share, :, columns].reshape(share * SLOTS, depth)
            gate_sum[...] += jnp.dot(rows, gate_w[own, columns, :], preferred_element_type=jnp.float32)
            up_sum[...] += jnp.dot(rows, up_w[own, columns, :], preferred_element_type=jnp.float32)
            return 0

        lax.fori_loop(0, WIDTH // depth, multiply, 0)

        def finish(at, _):
            rows = pl.ds(pl.multiple_of(at * SLOTS, SLOTS), SLOTS)
            value = gate_sum[rows]
            there = pl.ds(pl.multiple_of((wave * share + at) * SLOTS, SLOTS), SLOTS)
            act_ref[own, there] = (value / (1.0 + jnp.exp(-value)) * up_sum[rows] * scales[own, wave * share + at][:, :1]).astype(jnp.bfloat16)
            return 0

        lax.fori_loop(0, share, finish, 0)

    def settle(wave):
        for (part, _, _), copy in pair.items():
            if part // 3 == wave:
                copy.wait_recv()
        lax.fori_loop(wave * share, (wave + 1) * share, choose, 0)

    send_near(0, 0)
    send_near(1, 0)
    for load in loads:
        load.start()
    send_far(0, 0)
    take_far(0, 0)
    send_near(0, 1)
    send_far(1, 0)
    take_far(1, 0)
    send_near(1, 1)
    send_far(0, 1)
    take_far(0, 1)
    send_near(0, 2)
    send_far(1, 1)
    take_far(1, 1)
    send_near(1, 2)
    send_far(0, 2)
    take_far(0, 2)
    settle(0)
    send_far(1, 2)
    for load in loads:
        load.wait()
    open_one(0, 0)
    open_one(0, 1)
    take_far(1, 2)
    settle(1)
    open_one(1, 0)
    open_one(1, 1)
    for copy in [first, *near.values(), *far.values(), *pair.values()]:
        copy.wait_send()


def gather_and_open(mine, w_gate, w_up):
    bf16, f32, dma = jnp.bfloat16, jnp.float32, pltpu.SemaphoreType.DMA
    groups, span = 2 * SIDE, SIDE * SIDE * BLOCK
    hidden = w_gate.shape[2]
    vmem, hbm = pl.BlockSpec(memory_space=pltpu.VMEM), pl.BlockSpec(memory_space=pl.ANY)
    parts = len(PARTS)
    return pl.pallas_call(
        open_kernel,
        out_shape=(
            jax.ShapeDtypeStruct((2, groups * SLOTS, hidden), bf16),
            jax.ShapeDtypeStruct((groups, span, 128), bf16),
        ),
        in_specs=[vmem, hbm, hbm],
        out_specs=(vmem, vmem),
        scratch_shapes=[
            pltpu.VMEM((2, SIDE, SIDE, SIDE, *mine.shape), bf16),
            pltpu.VMEM(w_gate.shape, bf16),
            pltpu.VMEM(w_up.shape, bf16),
            pltpu.VMEM((2, groups, SLOTS, WIDTH), bf16),
            pltpu.VMEM((2, groups, SLOTS, 128), f32),
            pltpu.VMEM((groups // 2 * SLOTS, hidden), f32),
            pltpu.VMEM((groups // 2 * SLOTS, hidden), f32),
            dma, dma((2,)),
            dma((parts, 3, 2)), dma((parts, 3, 2)), dma((parts, 3, 2)), dma((parts, 3, 2)),
            dma((parts, 3, 3)), dma((parts, 3, 3)), dma, dma,
        ],
        compiler_params=pltpu.CompilerParams(collective_id=1, has_side_effects=True, vmem_limit_bytes=60 * 1024 * 1024),
    )(mine, w_gate, w_up)

def close_kernel(act_ref, pick_ref, down_ref, out_ref, acc, pair_buf, down_w, result,
                 near0, near1, near2, far0, far1, far2,
                 weight_sem, pair_send, pair_recv, near_send, near_recv, far_send, far_recv):
    me = my_place()
    core = me["c"]
    sibling = sibling_of(me)
    near_bufs, far_bufs = (near0, near1, near2), (far0, far1, far2)
    loads = []
    for part in range(len(PARTS)):
        start, size = columns_of(TILES_BACK, part)
        columns = (slice(None), slice(None), pl.ds(start, size))
        loads.append(pltpu.make_async_copy(down_ref.at[columns], down_w.at[columns], weight_sem.at[part]))
        loads[-1].start()
    greet([sibling] + [shifted(me, axis, by) for axis in "xyz" for by in (1, 2, 3)])
    pair, near, far = {}, {}, {}
    groups, span = pick_ref.shape[0], pick_ref.shape[1]

    def axis_of(part, stage):
        return PARTS[part][2 - stage]

    def group(ref, part, stage, shift, which, halves=None):
        place = shifted(me, axis_of(part, stage), shift)
        return blocks_at(ref, which, place, PARTS[part][: 2 - stage], halves, columns_of(TILES_BACK, part))

    def multiply(part):
        loads[part].wait()
        start, size = columns_of(TILES_BACK, part)
        for own in range(2):
            product = jnp.dot(act_ref[own], down_w[own, :, start : start + size], preferred_element_type=jnp.float32)
            result[:, own, :, :size] = product.astype(jnp.bfloat16).reshape(groups, SLOTS, size)

        def spread(at, _):
            both = result[at, :, :, :size].reshape(2 * SLOTS, size)
            rows = jnp.dot(pick_ref[at], both, preferred_element_type=jnp.float32).astype(jnp.bfloat16)
            acc[at // SIDE, at % SIDE, :, :, :, start : start + size] = rows.reshape(SIDE, SIDE, BLOCK, size)
            return 0

        lax.fori_loop(0, groups, spread, 0)
        for number, shift in enumerate((2, 1, -1, 0)):
            copy = remote(
                group(acc, part, 0, shift, 1 - core), group(pair_buf, part, 0, shift, 0),
                pair_send.at[part, number], pair_recv.at[part, number], sibling,
            )
            copy.start()
            pair[part, number] = copy

    def add_into(target, others):
        lead = target.shape[:-2]
        count = math.prod(lead)

        def body(at, _):
            index = []
            rest = at
            for size in reversed(lead):
                index.insert(0, rest % size)
                rest = rest // size
            index = (*index, slice(None), slice(None))
            total = target[index].astype(jnp.float32)
            for other in others:
                total += other[index].astype(jnp.float32)
            target[index] = total.astype(target.dtype)
            return 0

        if count == 1:
            body(0, 0)
        else:
            lax.fori_loop(0, count, body, 0)

    def add_pair(part, number, shift):
        pair[part, number].wait_recv()
        add_into(group(acc, part, 0, shift, core), [group(pair_buf, part, 0, shift, 0)])

    def near_copy(part, stage, way, half):
        by = 1 if way == 0 else -1
        src = group(acc, part, stage, by, core, half)
        dst = near_bufs[stage].at[part, way, half, ..., pl.ds(0, src.shape[-1])]
        copy = remote(src, dst, near_send.at[part, stage, way, half], near_recv.at[part, stage, way, half], shifted(me, axis_of(part, stage), by))
        copy.start()
        near[part, stage, way, half] = copy

    def send_far(wave, stage):
        for part in range(3 * wave, 3 * wave + 3):
            if stage == 0:
                add_pair(part, 0, 2)
            for way, by in ((0, 1), (1, -1)):
                src = group(acc, part, stage, 2, core, way)
                dst = far_bufs[stage].at[part, way, ..., pl.ds(0, src.shape[-1])]
                by = 2 if (wave, stage) in DIRECT_BACK else by
                copy = remote(src, dst, far_send.at[part, stage, way], far_recv.at[part, stage, way], shifted(me, axis_of(part, stage), by))
                copy.start()
                far[part, stage, way] = copy

    def send_near(wave, stage):
        for part in range(3 * wave, 3 * wave + 3):
            for way, by in ((0, 1), (1, -1)):
                if stage == 0:
                    add_pair(part, 1 + way, by)
                near_copy(part, stage, way, 1 - way)
                if (wave, stage) in DIRECT_BACK:
                    near_copy(part, stage, way, way)

    def relay(wave, stage):
        if (wave, stage) in DIRECT_BACK:
            return
        for part in range(3 * wave, 3 * wave + 3):
            for way, by in ((0, 1), (1, -1)):
                far[part, stage, way].wait_recv()
                target = group(acc, part, stage, by, core, way)
                add_into(target, [far_bufs[stage].at[part, way, ..., pl.ds(0, target.shape[-1])]])
                near_copy(part, stage, way, way)

    def take(wave, stage):
        for part in range(3 * wave, 3 * wave + 3):
            if stage == 0:
                add_pair(part, 3, 0)
            for half in (0, 1):
                for way in (0, 1):
                    near[part, stage, way, half].wait_recv()
                target = group(acc, part, stage, 0, core, half)
                others = [near_bufs[stage].at[part, way, half, ..., pl.ds(0, target.shape[-1])] for way in (0, 1)]
                if (wave, stage) in DIRECT_BACK:
                    far[part, stage, half].wait_recv()
                    others.append(far_bufs[stage].at[part, half, ..., pl.ds(0, target.shape[-1])])
                if stage < 2:
                    add_into(target, others)
                else:
                    total = target[...].astype(jnp.float32)
                    for other in others:
                        total += other[...].astype(jnp.float32)
                    start, size = columns_of(TILES_BACK, part)
                    low = (size // 256) * 128
                    start, size = (start, low) if half == 0 else (start + low, size - low)
                    out_ref[:, pl.ds(start, size)] = total

    for part in range(3):
        multiply(part)
    send_far(0, 0)
    send_near(0, 0)
    for part in range(3, 6):
        multiply(part)
    relay(0, 0)
    send_far(1, 0)
    send_near(1, 0)
    take(0, 0)
    send_far(0, 1)
    send_near(0, 1)
    relay(1, 0)
    relay(0, 1)
    take(0, 1)
    send_far(0, 2)
    send_near(0, 2)
    take(1, 0)
    send_far(1, 1)
    send_near(1, 1)
    relay(0, 2)
    relay(1, 1)
    take(0, 2)
    take(1, 1)
    send_far(1, 2)
    send_near(1, 2)
    relay(1, 2)
    take(1, 2)
    for copy in [*pair.values(), *near.values(), *far.values()]:
        copy.wait_send()


def close_and_reduce(act, pick, w_down):
    bf16, dma = jnp.bfloat16, pltpu.SemaphoreType.DMA
    groups = pick.shape[0]
    half = SIDE // 2
    parts = len(PARTS)
    last = WIDEST // 2
    vmem, hbm = pl.BlockSpec(memory_space=pltpu.VMEM), pl.BlockSpec(memory_space=pl.ANY)
    return pl.pallas_call(
        close_kernel,
        out_shape=jax.ShapeDtypeStruct((BLOCK, WIDTH), jnp.float32),
        in_specs=[vmem, vmem, hbm],
        out_specs=vmem,
        scratch_shapes=[
            pltpu.VMEM((2, SIDE, SIDE, SIDE, BLOCK, WIDTH), bf16),
            pltpu.VMEM((1, SIDE, SIDE, SIDE, BLOCK, WIDTH), bf16),
            pltpu.VMEM(w_down.shape, bf16),
            pltpu.VMEM((groups, 2, SLOTS, WIDEST), bf16),
            pltpu.VMEM((parts, 2, 2, SIDE, half, BLOCK, WIDEST), bf16),
            pltpu.VMEM((parts, 2, 2, half, BLOCK, WIDEST), bf16),
            pltpu.VMEM((parts, 2, 2, BLOCK, last), bf16),
            pltpu.VMEM((parts, 2, SIDE, half, BLOCK, WIDEST), bf16),
            pltpu.VMEM((parts, 2, half, BLOCK, WIDEST), bf16),
            pltpu.VMEM((parts, 2, BLOCK, last), bf16),
            dma((parts,)), dma((parts, 4)), dma((parts, 4)),
            dma((parts, 3, 2, 2)), dma((parts, 3, 2, 2)), dma((parts, 3, 2)), dma((parts, 3, 2)),
        ],
        compiler_params=pltpu.CompilerParams(collective_id=2, has_side_effects=True, vmem_limit_bytes=60 * 1024 * 1024),
    )(act, pick, w_down)


def on_device(
    queries,
    new_keys,
    new_values,
    key_cache,
    value_cache,
    cache_lengths,
    out_weight,
    residual_in,
    norm_gain,
    expert_ids,
    route_weights,
    w_gate,
    w_up,
    w_down,
):
    hidden_one, normed = attend_and_project(
        queries, new_keys, new_values, key_cache, value_cache, cache_lengths, out_weight, residual_in, norm_gain,
        expert_ids, route_weights,
    )
    act, pick = gather_and_open(normed, w_gate, w_up)
    return (hidden_one + close_and_reduce(act, pick, w_down)).astype(jnp.bfloat16)


def solution(mesh):
    in_specs = (
        P("dp", "head"),
        P("dp", "head"),
        P("dp", "head"),
        P("dp", "head", None, None),
        P("dp", "head", None, None),
        P("dp"),
        P("head", "dp"),
        P(("dp", "head"), None),
        P(),
        P(("dp", "head"), None),
        P(("dp", "head"), None),
        P("dp", None, "head"),
        P("dp", None, "head"),
        P("dp", "head", None),
    )
    out_specs = P(("dp", "head"), None)
    return jax.shard_map(
        on_device, mesh=mesh, in_specs=in_specs, out_specs=out_specs, check_vma=False
    )
```

```python
import math

import jax
import jax.numpy as jnp
from jax import lax
from jax.experimental import pallas as pl
from jax.experimental.pallas import tpu as pltpu
from jax.sharding import PartitionSpec as P

MESH = pl.DeviceIdType.MESH
SIDE = 4
WIDTH = 4096
BLOCK = 16
CAPACITY = 4
CHOICES = 8
SLOTS = 64
ORDERS = (("x", "y", "z"), ("y", "z", "x"), ("z", "x", "y"))
WAVES = 2
PARTS = ORDERS * WAVES
WIDE = WIDTH + 256
TILES_OUT = (6, 6, 5)
TILES_BACK = (6, 6, 6, 5, 5, 4)
DIRECT_OUT = ((0, 0), (0, 1))
DIRECT_BACK = ((1, 1), (1, 2))
WIDEST = 768


def columns_of(tiles, part):
    return 128 * sum(tiles[:part]), 128 * tiles[part]


def my_place():
    row = lax.axis_index("dp")
    return {
        "y": row // (2 * SIDE),
        "x": (row // 2) % SIDE,
        "c": row % 2,
        "z": lax.axis_index("head"),
    }


def device_of(place):
    return ((place["y"] * SIDE + place["x"]) * 2 + place["c"], place["z"])


def shifted(place, axis, by):
    other = dict(place)
    other[axis] = (place[axis] + by) % SIDE
    return other


def sibling_of(place):
    other = dict(place)
    other["c"] = 1 - place["c"]
    return other


def greet(partners):
    barrier = pltpu.get_barrier_semaphore()
    for partner in partners:
        pl.semaphore_signal(barrier, inc=1, device_id=device_of(partner), device_id_type=MESH)
    pl.semaphore_wait(barrier, len(partners))


def remote(src, dst, send, recv, place):
    return pltpu.make_async_remote_copy(
        src_ref=src, dst_ref=dst, send_sem=send, recv_sem=recv,
        device_id=device_of(place), device_id_type=MESH,
    )


def blocks_at(ref, core, place, free, halves, columns):
    index = [core]
    last = max(free, key="zyx".index, default=None)
    for axis in ("z", "y", "x"):
        if axis in free:
            if halves is not None and axis == last:
                index.append(pl.ds(halves * (SIDE // 2), SIDE // 2))
            else:
                index.append(slice(None))
        else:
            index.append(place[axis])
    start, size = columns
    if not free and halves is not None:
        low = (size // 256) * 128
        start, size = (start, low) if halves == 0 else (start + low, size - low)
    return ref.at[(*index, slice(None), pl.ds(start, size))]


def attend_rows(base, rows, lengths_ref, query_ref, fresh_key_ref, fresh_value_ref, keys, values, attn_ref):
    slots, head_size = keys.shape[1:]
    heads = query_ref.shape[1] // head_size
    factor = 1.0 / math.sqrt(head_size)
    slot = lax.broadcasted_iota(jnp.int32, (heads, slots), 1)
    block = pl.ds(base, rows)
    query = jnp.stack([query_ref[block, head * head_size : (head + 1) * head_size].astype(jnp.float32) for head in range(heads)])
    query = jnp.swapaxes(query, 0, 1)
    narrow = query.astype(jnp.bfloat16)
    scores = []
    for row in range(rows):
        score = lax.dot_general(narrow[row], keys[base + row], (((1,), (1,)), ((), ())), preferred_element_type=jnp.float32)
        scores.append(jnp.where(slot < lengths_ref[base + row], score * factor, -1e30))
    scores = jnp.concatenate(scores, axis=0)
    fresh_key = fresh_key_ref[block].astype(jnp.float32).reshape(rows, 1, head_size)
    fresh = jnp.sum(query * fresh_key, axis=-1, keepdims=True).reshape(rows * heads, 1) * factor
    highest = jnp.maximum(jnp.max(scores, axis=-1, keepdims=True), fresh)
    spread = jnp.exp(scores - highest)
    fresh_exp = jnp.exp(fresh - highest)
    inverse = 1.0 / (jnp.sum(spread, axis=-1, keepdims=True) + fresh_exp)
    weights = (spread * inverse).astype(jnp.bfloat16)
    fresh_weight = (fresh_exp * inverse).astype(jnp.bfloat16).astype(jnp.float32)
    mixed = [
        jnp.dot(weights[row * heads : (row + 1) * heads], values[base + row], preferred_element_type=jnp.float32)
        for row in range(rows)
    ]
    fresh_value = fresh_value_ref[block].astype(jnp.float32).reshape(rows, 1, head_size)
    mixed = jnp.concatenate(mixed, axis=0).reshape(rows, heads, head_size) + fresh_weight.reshape(rows, heads, 1) * fresh_value
    mixed = jnp.swapaxes(mixed, 0, 1).astype(jnp.bfloat16)
    for head in range(heads):
        attn_ref[block, head * head_size : (head + 1) * head_size] = mixed[head]


def route_block(names_ref, names, weights, table):
    choices, rows = names.shape
    lane = lax.broadcasted_iota(jnp.int32, (choices, rows), 1)
    position = jnp.zeros((choices, rows), jnp.int32)
    for row in range(rows):
        same = names == names_ref[0, row]
        for choice in range(1, choices):
            same = same | (names == names_ref[choice, row])
        position += jnp.where(same & (lane > row), 1, 0)
    gates = weights / jnp.sum(weights, axis=0, keepdims=True)
    upper = gates.astype(jnp.bfloat16).astype(jnp.float32)
    table[...] = jnp.zeros_like(table)
    table[0:choices, 0:rows] = (names * CAPACITY + position).astype(jnp.float32)
    table[choices : 2 * choices, 0:rows] = upper
    table[2 * choices : 3 * choices, 0:rows] = gates - upper
    return table[...].T[0:rows].astype(jnp.bfloat16)


def attend_and_project_kernel(lengths_ref, names_ref, query_in, fresh_key_in, fresh_value_in, key_ref, value_ref,
                              weight_ref, residual_in, gain_in, names_in, weights_in, hidden_ref, normed_ref,
                              query_ref, fresh_key_ref, fresh_value_ref, residual_ref, gain_ref, names_here, weights_here, table,
                              attn_ref, keys, values, attn_all, weight_all, sums, sums_in, mine, mine_in,
                   local_sem, input_sem, key_sem, value_sem, w_send, w_recv, a_send, a_recv, f_send, f_recv, p_send, p_recv, s_send, s_recv, m_send, m_recv):
    me = my_place()
    sibling = sibling_of(me)
    rows, depth = attn_ref.shape
    inputs = [
        pltpu.make_async_copy(src, dst, input_sem.at[at])
        for at, (src, dst) in enumerate((
            (query_in, query_ref), (fresh_key_in, fresh_key_ref), (fresh_value_in, fresh_value_ref), (residual_in, residual_ref),
            (gain_in, gain_ref), (names_in, names_here), (weights_in, weights_here),
        ))
    ]
    for load in inputs:
        load.start()
    own_cols = weight_ref.shape[1]
    half_depth, half_rows = depth // 2, rows // 2
    step = 16
    loads = []
    for at in range(rows // step):
        block = pl.ds(at * step, step)
        loads.append((pltpu.make_async_copy(key_ref.at[block, 0], keys.at[block], key_sem.at[at]),
                      pltpu.make_async_copy(value_ref.at[block, 0], values.at[block], value_sem.at[at])))
        for load in loads[-1]:
            load.start()

    def neighbour(by, core):
        other = shifted(me, "x", by)
        other["c"] = (me["c"] + core) % 2
        return other

    others = [(by, core) for by in range(SIDE) for core in range(2) if by or core]
    greet([neighbour(*which) for which in others] + [shifted(me, axis, by) for axis in "yz" for by in (1, 2, 3)])

    def weight_at(by, low=0, size=depth):
        column = ((me["y"] + by) % SIDE) * own_cols
        return weight_all.at[pl.ds(low, size), pl.ds(pl.multiple_of(column, own_cols), own_cols)]

    def attn_at(by, core, low=0, size=rows):
        return attn_all.at[(me["x"] + by) % SIDE, core, pl.ds(low, size)]

    core = me["c"]
    own_w = pltpu.make_async_copy(weight_ref, weight_at(0), local_sem.at[0])
    own_w.start()
    started = []

    def go(src, dst, send, recv, place):
        copy = remote(src, dst, send, recv, place)
        copy.start()
        started.append(copy)
        return copy

    near_w, near_a, far_w, far_a, pair = {}, {}, {}, {}, {}
    for way, by in ((0, 1), (1, -1)):
        near_w[way] = go(weight_ref, weight_at(0), w_send.at[way], w_recv.at[way], shifted(me, "y", by))
    for load in inputs:
        load.wait()
    def send_attn(half):
        src, dst = attn_ref.at[pl.ds(half * half_rows, half_rows)], attn_at(0, core, half * half_rows, half_rows)
        for way, by in ((0, 1), (1, -1)):
            near_a[way, half] = go(src, dst, a_send.at[way, half], a_recv.at[way, half], shifted(me, "x", by))
        pair[0, half] = go(src, dst, p_send.at[0, half], p_recv.at[0, half], sibling)

    def pass_attn(way, by, half):
        near_a[way, half].wait_recv()
        block = attn_at(-by, core, half * half_rows, half_rows)
        if way == half:
            far_a[way] = go(block, block, f_send.at[way], f_recv.at[way], shifted(me, "x", by))
        pair[-by, half] = go(block, block, p_send.at[1 + way, half], p_recv.at[1 + way, half], sibling)

    chunks = rows // step
    for at in range(chunks):
        for load in loads[at]:
            load.wait()
        attend_rows(at * step, step, lengths_ref, query_ref, fresh_key_ref, fresh_value_ref, keys, values, attn_ref)
        if at == chunks // 2 - 1:
            send_attn(0)
    send_attn(1)
    own_a = pltpu.make_async_copy(attn_ref, attn_at(0, core), local_sem.at[1])
    own_a.start()
    for way, by in ((0, 1), (1, -1)):
        near_w[way].wait_recv()
        block = weight_at(-by, way * half_depth, half_depth)
        far_w[way] = go(block, block, w_send.at[2 + way], w_recv.at[2 + way], shifted(me, "y", by))
    for half in (0, 1):
        for way, by in ((0, 1), (1, -1)):
            pass_attn(way, by, half)
    for way in (0, 1):
        far_a[way].wait_recv()
        block = attn_at(2, core, way * half_rows, half_rows)
        pair[2, way] = go(block, block, p_send.at[3, way], p_recv.at[3, way], sibling)
    normed_ref[:, WIDTH : WIDTH + 128] = route_block(names_ref, names_here[...], weights_here[...], table)
    normed_ref[:, WIDTH + 128 :] = jnp.zeros((rows // SIDE, WIDE - WIDTH - 128), normed_ref.dtype)
    own_w.wait()
    own_a.wait()
    for way in (0, 1):
        far_w[way].wait_recv()

    share = rows // SIDE
    width = weight_all.shape[1]
    order = (0, 1, -1, 2)
    to_head = {}
    for number, by in enumerate(order):
        for half in (0, 1):
            pair[by, half].wait_recv()
        at = (me["x"] + by) % SIDE
        block = attn_all[at].reshape(2 * rows, depth)
        part = jnp.dot(block, weight_all[...], preferred_element_type=jnp.float32).astype(jnp.bfloat16)
        part = part.reshape(2, SIDE, share, width)
        for head in range(SIDE):
            sums[head, at] = part[:, head]
        for away in (1, 2, 3):
            target = shifted(me, "z", away)
            to_head[number, away] = go(sums.at[target["z"], at], sums_in.at[away - 1, at],
                                       s_send.at[number, away - 1], s_recv.at[number, away - 1], target)
    slots = {}
    for number, by in enumerate(order):
        at = (me["x"] + by) % SIDE
        for away in (1, 2, 3):
            to_head[number, away].wait_recv()
        total = sums[me["z"], at].astype(jnp.float32)
        for away in range(3):
            total += sums_in[away, at].astype(jnp.float32)
        mine[number] = total.astype(jnp.bfloat16)
        for flip in (0, 1):
            if by == 0 and flip == 0:
                continue
            target = neighbour(by, flip)
            slots[number, flip] = go(mine.at[number, target["c"]], mine_in.at[me["x"], core],
                                     m_send.at[number, flip], m_recv.at[number, flip], target)
    keep = pltpu.make_async_copy(mine.at[0, core], mine_in.at[me["x"], core], local_sem.at[2])
    keep.start()
    keep.wait()
    for copy in slots.values():
        copy.wait_recv()
    square = jnp.zeros((share, 1), jnp.float32)
    for y in range(SIDE):
        for x in range(SIDE):
            for c in range(2):
                start = ((y * SIDE + x) * 2 + c) * own_cols
                value = residual_ref[:, start : start + own_cols].astype(jnp.float32)
                value += mine_in[x, c, :, y * own_cols : (y + 1) * own_cols].astype(jnp.float32)
                hidden_ref[:, start : start + own_cols] = value
                square += jnp.sum(value * value, axis=-1, keepdims=True)
    scale = lax.rsqrt(square / WIDTH + 1e-06)
    for start in range(0, WIDTH, 512):
        normed_ref[:, start : start + 512] = (hidden_ref[:, start : start + 512] * scale * gain_ref[:, start : start + 512]).astype(jnp.bfloat16)
    for copy in started:
        copy.wait_send()


def attend_and_project(queries, new_keys, new_values, key_cache, value_cache, cache_lengths, out_weight, residual, gain, expert_ids, route_weights):
    rows, _, slots, head_size = key_cache.shape
    depth = queries.shape[1]
    own_cols = out_weight.shape[1]
    width = SIDE * own_cols
    share = rows // SIDE
    vmem, hbm, smem = (pl.BlockSpec(memory_space=space) for space in (pltpu.VMEM, pl.ANY, pltpu.SMEM))
    names, route_weights = expert_ids.T, route_weights.T
    bf16 = jnp.bfloat16
    dma = pltpu.SemaphoreType.DMA
    return pl.pallas_call(
        attend_and_project_kernel,
        out_shape=(
            jax.ShapeDtypeStruct((share, WIDTH), jnp.float32),
            jax.ShapeDtypeStruct((share, WIDE), bf16),
        ),
        in_specs=[smem, smem] + [hbm] * 10,
        out_specs=(vmem, vmem),
        scratch_shapes=[
            pltpu.VMEM((rows, depth), bf16),
            pltpu.VMEM(new_keys.shape, bf16),
            pltpu.VMEM(new_values.shape, bf16),
            pltpu.VMEM(residual.shape, bf16),
            pltpu.VMEM((1, WIDTH), jnp.float32),
            pltpu.VMEM(names.shape, jnp.int32),
            pltpu.VMEM(names.shape, jnp.float32),
            pltpu.VMEM((128, 128), jnp.float32),
            pltpu.VMEM((rows, depth), bf16),
            pltpu.VMEM((rows, slots, head_size), bf16),
            pltpu.VMEM((rows, slots, head_size), bf16),
            pltpu.VMEM((SIDE, 2, rows, depth), bf16),
            pltpu.VMEM((depth, width), bf16),
            pltpu.VMEM((SIDE, SIDE, 2, share, width), bf16),
            pltpu.VMEM((SIDE - 1, SIDE, 2, share, width), bf16),
            pltpu.VMEM((SIDE, 2, share, width), bf16),
            pltpu.VMEM((SIDE, 2, share, width), bf16),
            dma((3,)), dma((7,)), dma((rows // 16,)), dma((rows // 16,)),
            dma((4,)), dma((4,)), dma((2, 2)), dma((2, 2)), dma((2,)), dma((2,)), dma((4, 2)), dma((4, 2)),
            dma((4, 3)), dma((4, 3)), dma((4, 2)), dma((4, 2)),
        ],
        compiler_params=pltpu.CompilerParams(collective_id=3, has_side_effects=True, vmem_limit_bytes=60 * 1024 * 1024),
    )(cache_lengths, names, queries, new_keys, new_values, key_cache, value_cache, out_weight, residual, gain.reshape(1, WIDTH), names, route_weights)


def pick_group(table):
    span = table.shape[0]
    lane = lax.broadcasted_iota(jnp.int32, table.shape, 1)
    row = lax.broadcasted_iota(jnp.int32, (span, 1), 0)
    place = (row // BLOCK * CAPACITY).astype(jnp.float32)
    first = (lax.axis_index("dp") * 2 * CAPACITY).astype(jnp.float32)
    spot = lane.astype(jnp.float32)
    picked = jnp.zeros(table.shape, jnp.float32)
    gates = jnp.zeros(table.shape, jnp.float32)
    for own in range(2):
        code = table - (first + own * CAPACITY)
        hit = jnp.where((lane < CHOICES) & (code >= 0) & (code < CAPACITY), 1.0, 0.0)
        slot = jnp.sum(hit * (code + 1), axis=-1, keepdims=True)
        slot = jnp.where(slot > 0, slot - 1 + place + own * SLOTS, -1.0)
        gate = jnp.sum(table * (pltpu.roll(hit, CHOICES, 1) + pltpu.roll(hit, 2 * CHOICES, 1)), axis=-1, keepdims=True)
        match = spot == slot
        picked += jnp.where(match, 1.0, 0.0)
        gates += jnp.where(match, gate, 0.0)
    scale = jnp.broadcast_to(jnp.sum(gates, axis=0, keepdims=True), (128, 128)).T
    return picked, scale


def open_kernel(mine_ref, gate_ref, up_ref, act_ref, pick_ref, everyone, gate_w, up_w, chosen, scales, gate_sum, up_sum,
                own_sem, weight_sem, near_send, near_recv, far_send, far_recv, pair_send, pair_recv, first_send, first_recv):
    me = my_place()
    core = me["c"]
    sibling = sibling_of(me)
    loads = [pltpu.make_async_copy(gate_ref, gate_w, weight_sem.at[0]), pltpu.make_async_copy(up_ref, up_w, weight_sem.at[1])]
    greet([sibling] + [shifted(me, axis, by) for axis in "xyz" for by in (1, 2, 3)])
    home = everyone.at[core, me["z"], me["y"], me["x"]]
    own = pltpu.make_async_copy(mine_ref, home, own_sem)
    own.start()
    first = remote(mine_ref, home, first_send, first_recv, sibling)
    first.start()
    own.wait()
    first.wait_recv()
    near, far, pair = {}, {}, {}

    def group(part, stage, coordinate_shift, halves=None):
        order = PARTS[part]
        place = shifted(me, order[stage], coordinate_shift)
        start, size = columns_of(TILES_OUT, part % 3)
        start = pl.multiple_of(core * (WIDE // 2) + start, 128)
        return blocks_at(everyone, part // 3, place, order[:stage], halves, (start, size))

    def to_pair(part, stage, number, block):
        copy = remote(block, block, pair_send.at[part, stage, number], pair_recv.at[part, stage, number], sibling)
        copy.start()
        pair[part, stage, number] = copy

    def send_near(wave, stage):
        for part in range(3 * wave, 3 * wave + 3):
            block = group(part, stage, 0)
            if (wave, stage) in DIRECT_OUT:
                copy = remote(block, block, far_send.at[part, stage, 0], far_recv.at[part, stage, 0], shifted(me, PARTS[part][stage], 2))
                copy.start()
                far[part, stage, 0] = copy
            for way, by in ((0, 1), (1, -1)):
                copy = remote(block, block, near_send.at[part, stage, way], near_recv.at[part, stage, way], shifted(me, PARTS[part][stage], by))
                copy.start()
                near[part, stage, way] = copy

    def send_far(wave, stage):
        for part in range(3 * wave, 3 * wave + 3):
            for way, by in ((0, 1), (1, -1)):
                near[part, stage, way].wait_recv()
                if (wave, stage) not in DIRECT_OUT:
                    block = group(part, stage, -by, way)
                    copy = remote(block, block, far_send.at[part, stage, way], far_recv.at[part, stage, way], shifted(me, PARTS[part][stage], by))
                    copy.start()
                    far[part, stage, way] = copy
                to_pair(part, stage, way, group(part, stage, -by))

    def take_far(wave, stage):
        for part in range(3 * wave, 3 * wave + 3):
            for way in (0, 1):
                if (part, stage, way) in far:
                    far[part, stage, way].wait_recv()
            to_pair(part, stage, 2, group(part, stage, 2))

    groups, span = pick_ref.shape[0], pick_ref.shape[1]

    def choose(at, _):
        c, z = at // SIDE, at % SIDE
        picked, scale = pick_group(everyone[c, z, :, :, :, WIDTH : WIDTH + 128].reshape(span, 128).astype(jnp.float32))
        pick_ref[at] = picked.astype(jnp.bfloat16)
        turned = picked.T.astype(jnp.bfloat16)
        for half in range(2):
            scales[half, at] = scale[half * SLOTS : half * SLOTS + SLOTS]
        for start in range(0, WIDTH, 512):
            rows = everyone[c, z, :, :, :, start : start + 512].reshape(span, 512)
            part = jnp.dot(turned, rows, preferred_element_type=jnp.float32).astype(jnp.bfloat16)
            for half in range(2):
                chosen[half, at, :, start : start + 512] = part[half * SLOTS : half * SLOTS + SLOTS]
        return 0

    depth = 1024
    share = groups // 2

    def open_one(wave, own):
        gate_sum[...] = jnp.zeros_like(gate_sum)
        up_sum[...] = jnp.zeros_like(up_sum)

        def multiply(step, _):
            columns = pl.ds(pl.multiple_of(step * depth, depth), depth)
            rows = chosen[own, wave * share : (wave + 1) * share, :, columns].reshape(share * SLOTS, depth)
            gate_sum[...] += jnp.dot(rows, gate_w[own, columns, :], preferred_element_type=jnp.float32)
            up_sum[...] += jnp.dot(rows, up_w[own, columns, :], preferred_element_type=jnp.float32)
            return 0

        lax.fori_loop(0, WIDTH // depth, multiply, 0)

        def finish(at, _):
            rows = pl.ds(pl.multiple_of(at * SLOTS, SLOTS), SLOTS)
            value = gate_sum[rows]
            there = pl.ds(pl.multiple_of((wave * share + at) * SLOTS, SLOTS), SLOTS)
            act_ref[own, there] = (value / (1.0 + jnp.exp(-value)) * up_sum[rows] * scales[own, wave * share + at][:, :1]).astype(jnp.bfloat16)
            return 0

        lax.fori_loop(0, share, finish, 0)

    def settle(wave):
        for (part, _, _), copy in pair.items():
            if part // 3 == wave:
                copy.wait_recv()
        lax.fori_loop(wave * share, (wave + 1) * share, choose, 0)

    send_near(0, 0)
    send_near(1, 0)
    for load in loads:
        load.start()
    send_far(0, 0)
    take_far(0, 0)
    send_near(0, 1)
    send_far(1, 0)
    take_far(1, 0)
    send_near(1, 1)
    send_far(0, 1)
    take_far(0, 1)
    send_near(0, 2)
    send_far(1, 1)
    take_far(1, 1)
    send_far(0, 2)
    send_near(1, 2)
    take_far(0, 2)
    settle(0)
    send_far(1, 2)
    for load in loads:
        load.wait()
    open_one(0, 0)
    open_one(0, 1)
    take_far(1, 2)
    settle(1)
    open_one(1, 0)
    open_one(1, 1)
    for copy in [first, *near.values(), *far.values(), *pair.values()]:
        copy.wait_send()


def gather_and_open(mine, w_gate, w_up):
    bf16, f32, dma = jnp.bfloat16, jnp.float32, pltpu.SemaphoreType.DMA
    groups, span = 2 * SIDE, SIDE * SIDE * BLOCK
    hidden = w_gate.shape[2]
    vmem, hbm = pl.BlockSpec(memory_space=pltpu.VMEM), pl.BlockSpec(memory_space=pl.ANY)
    parts = len(PARTS)
    return pl.pallas_call(
        open_kernel,
        out_shape=(
            jax.ShapeDtypeStruct((2, groups * SLOTS, hidden), bf16),
            jax.ShapeDtypeStruct((groups, span, 128), bf16),
        ),
        in_specs=[vmem, hbm, hbm],
        out_specs=(vmem, vmem),
        scratch_shapes=[
            pltpu.VMEM((2, SIDE, SIDE, SIDE, *mine.shape), bf16),
            pltpu.VMEM(w_gate.shape, bf16),
            pltpu.VMEM(w_up.shape, bf16),
            pltpu.VMEM((2, groups, SLOTS, WIDTH), bf16),
            pltpu.VMEM((2, groups, SLOTS, 128), f32),
            pltpu.VMEM((groups // 2 * SLOTS, hidden), f32),
            pltpu.VMEM((groups // 2 * SLOTS, hidden), f32),
            dma, dma((2,)),
            dma((parts, 3, 2)), dma((parts, 3, 2)), dma((parts, 3, 2)), dma((parts, 3, 2)),
            dma((parts, 3, 3)), dma((parts, 3, 3)), dma, dma,
        ],
        compiler_params=pltpu.CompilerParams(collective_id=1, has_side_effects=True, vmem_limit_bytes=60 * 1024 * 1024),
    )(mine, w_gate, w_up)

def close_kernel(act_ref, pick_ref, down_ref, out_ref, acc, pair_buf, down_w, result,
                 near0, near1, near2, far0, far1, far2,
                 weight_sem, pair_send, pair_recv, near_send, near_recv, far_send, far_recv):
    me = my_place()
    core = me["c"]
    sibling = sibling_of(me)
    near_bufs, far_bufs = (near0, near1, near2), (far0, far1, far2)
    loads = []
    for part in range(len(PARTS)):
        start, size = columns_of(TILES_BACK, part)
        columns = (slice(None), slice(None), pl.ds(start, size))
        loads.append(pltpu.make_async_copy(down_ref.at[columns], down_w.at[columns], weight_sem.at[part]))
        loads[-1].start()
    greet([sibling] + [shifted(me, axis, by) for axis in "xyz" for by in (1, 2, 3)])
    pair, near, far = {}, {}, {}
    groups, span = pick_ref.shape[0], pick_ref.shape[1]

    def axis_of(part, stage):
        return PARTS[part][2 - stage]

    def group(ref, part, stage, shift, which, halves=None):
        place = shifted(me, axis_of(part, stage), shift)
        return blocks_at(ref, which, place, PARTS[part][: 2 - stage], halves, columns_of(TILES_BACK, part))

    def multiply(part):
        loads[part].wait()
        start, size = columns_of(TILES_BACK, part)
        for own in range(2):
            product = jnp.dot(act_ref[own], down_w[own, :, start : start + size], preferred_element_type=jnp.float32)
            result[:, own, :, :size] = product.astype(jnp.bfloat16).reshape(groups, SLOTS, size)

        def spread(at, _):
            both = result[at, :, :, :size].reshape(2 * SLOTS, size)
            rows = jnp.dot(pick_ref[at], both, preferred_element_type=jnp.float32).astype(jnp.bfloat16)
            acc[at // SIDE, at % SIDE, :, :, :, start : start + size] = rows.reshape(SIDE, SIDE, BLOCK, size)
            return 0

        lax.fori_loop(0, groups, spread, 0)
        for number, shift in enumerate((2, 1, -1, 0)):
            copy = remote(
                group(acc, part, 0, shift, 1 - core), group(pair_buf, part, 0, shift, 0),
                pair_send.at[part, number], pair_recv.at[part, number], sibling,
            )
            copy.start()
            pair[part, number] = copy

    def add_into(target, others):
        lead = target.shape[:-2]
        count = math.prod(lead)

        def body(at, _):
            index = []
            rest = at
            for size in reversed(lead):
                index.insert(0, rest % size)
                rest = rest // size
            index = (*index, slice(None), slice(None))
            total = target[index].astype(jnp.float32)
            for other in others:
                total += other[index].astype(jnp.float32)
            target[index] = total.astype(target.dtype)
            return 0

        if count == 1:
            body(0, 0)
        else:
            lax.fori_loop(0, count, body, 0)

    def add_pair(part, number, shift):
        pair[part, number].wait_recv()
        add_into(group(acc, part, 0, shift, core), [group(pair_buf, part, 0, shift, 0)])

    def near_copy(part, stage, way, half):
        by = 1 if way == 0 else -1
        src = group(acc, part, stage, by, core, half)
        dst = near_bufs[stage].at[part, way, half, ..., pl.ds(0, src.shape[-1])]
        copy = remote(src, dst, near_send.at[part, stage, way, half], near_recv.at[part, stage, way, half], shifted(me, axis_of(part, stage), by))
        copy.start()
        near[part, stage, way, half] = copy

    def send_far(wave, stage):
        for part in range(3 * wave, 3 * wave + 3):
            if stage == 0:
                add_pair(part, 0, 2)
            for way, by in ((0, 1), (1, -1)):
                src = group(acc, part, stage, 2, core, way)
                dst = far_bufs[stage].at[part, way, ..., pl.ds(0, src.shape[-1])]
                by = 2 if (wave, stage) in DIRECT_BACK else by
                copy = remote(src, dst, far_send.at[part, stage, way], far_recv.at[part, stage, way], shifted(me, axis_of(part, stage), by))
                copy.start()
                far[part, stage, way] = copy

    def send_near(wave, stage):
        for part in range(3 * wave, 3 * wave + 3):
            for way, by in ((0, 1), (1, -1)):
                if stage == 0:
                    add_pair(part, 1 + way, by)
                near_copy(part, stage, way, 1 - way)
                if (wave, stage) in DIRECT_BACK:
                    near_copy(part, stage, way, way)

    def relay(wave, stage):
        if (wave, stage) in DIRECT_BACK:
            return
        for part in range(3 * wave, 3 * wave + 3):
            for way, by in ((0, 1), (1, -1)):
                far[part, stage, way].wait_recv()
                target = group(acc, part, stage, by, core, way)
                add_into(target, [far_bufs[stage].at[part, way, ..., pl.ds(0, target.shape[-1])]])
                near_copy(part, stage, way, way)

    def take(wave, stage):
        for part in range(3 * wave, 3 * wave + 3):
            if stage == 0:
                add_pair(part, 3, 0)
            for half in (0, 1):
                for way in (0, 1):
                    near[part, stage, way, half].wait_recv()
                target = group(acc, part, stage, 0, core, half)
                others = [near_bufs[stage].at[part, way, half, ..., pl.ds(0, target.shape[-1])] for way in (0, 1)]
                if (wave, stage) in DIRECT_BACK:
                    far[part, stage, half].wait_recv()
                    others.append(far_bufs[stage].at[part, half, ..., pl.ds(0, target.shape[-1])])
                if stage < 2:
                    add_into(target, others)
                else:
                    total = target[...].astype(jnp.float32)
                    for other in others:
                        total += other[...].astype(jnp.float32)
                    start, size = columns_of(TILES_BACK, part)
                    low = (size // 256) * 128
                    start, size = (start, low) if half == 0 else (start + low, size - low)
                    out_ref[:, pl.ds(start, size)] = total

    for part in range(3):
        multiply(part)
    send_far(0, 0)
    send_near(0, 0)
    for part in range(3, 6):
        multiply(part)
    relay(0, 0)
    send_far(1, 0)
    send_near(1, 0)
    take(0, 0)
    send_far(0, 1)
    send_near(0, 1)
    relay(1, 0)
    relay(0, 1)
    take(0, 1)
    send_far(0, 2)
    send_near(0, 2)
    take(1, 0)
    send_far(1, 1)
    send_near(1, 1)
    relay(0, 2)
    relay(1, 1)
    take(0, 2)
    take(1, 1)
    send_far(1, 2)
    send_near(1, 2)
    relay(1, 2)
    take(1, 2)
    for copy in [*pair.values(), *near.values(), *far.values()]:
        copy.wait_send()


def close_and_reduce(act, pick, w_down):
    bf16, dma = jnp.bfloat16, pltpu.SemaphoreType.DMA
    groups = pick.shape[0]
    half = SIDE // 2
    parts = len(PARTS)
    last = WIDEST // 2
    vmem, hbm = pl.BlockSpec(memory_space=pltpu.VMEM), pl.BlockSpec(memory_space=pl.ANY)
    return pl.pallas_call(
        close_kernel,
        out_shape=jax.ShapeDtypeStruct((BLOCK, WIDTH), jnp.float32),
        in_specs=[vmem, vmem, hbm],
        out_specs=vmem,
        scratch_shapes=[
            pltpu.VMEM((2, SIDE, SIDE, SIDE, BLOCK, WIDTH), bf16),
            pltpu.VMEM((1, SIDE, SIDE, SIDE, BLOCK, WIDTH), bf16),
            pltpu.VMEM(w_down.shape, bf16),
            pltpu.VMEM((groups, 2, SLOTS, WIDEST), bf16),
            pltpu.VMEM((parts, 2, 2, SIDE, half, BLOCK, WIDEST), bf16),
            pltpu.VMEM((parts, 2, 2, half, BLOCK, WIDEST), bf16),
            pltpu.VMEM((parts, 2, 2, BLOCK, last), bf16),
            pltpu.VMEM((parts, 2, SIDE, half, BLOCK, WIDEST), bf16),
            pltpu.VMEM((parts, 2, half, BLOCK, WIDEST), bf16),
            pltpu.VMEM((parts, 2, BLOCK, last), bf16),
            dma((parts,)), dma((parts, 4)), dma((parts, 4)),
            dma((parts, 3, 2, 2)), dma((parts, 3, 2, 2)), dma((parts, 3, 2)), dma((parts, 3, 2)),
        ],
        compiler_params=pltpu.CompilerParams(collective_id=2, has_side_effects=True, vmem_limit_bytes=60 * 1024 * 1024),
    )(act, pick, w_down)


def on_device(
    queries,
    new_keys,
    new_values,
    key_cache,
    value_cache,
    cache_lengths,
    out_weight,
    residual_in,
    norm_gain,
    expert_ids,
    route_weights,
    w_gate,
    w_up,
    w_down,
):
    hidden_one, normed = attend_and_project(
        queries, new_keys, new_values, key_cache, value_cache, cache_lengths, out_weight, residual_in, norm_gain,
        expert_ids, route_weights,
    )
    act, pick = gather_and_open(normed, w_gate, w_up)
    return (hidden_one + close_and_reduce(act, pick, w_down)).astype(jnp.bfloat16)


def solution(mesh):
    in_specs = (
        P("dp", "head"),
        P("dp", "head"),
        P("dp", "head"),
        P("dp", "head", None, None),
        P("dp", "head", None, None),
        P("dp"),
        P("head", "dp"),
        P(("dp", "head"), None),
        P(),
        P(("dp", "head"), None),
        P(("dp", "head"), None),
        P("dp", None, "head"),
        P("dp", None, "head"),
        P("dp", "head", None),
    )
    out_specs = P(("dp", "head"), None)
    return jax.shard_map(
        on_device, mesh=mesh, in_specs=in_specs, out_specs=out_specs, check_vma=False
    )
```

```python
import math

import jax
import jax.numpy as jnp
from jax import lax
from jax.experimental import pallas as pl
from jax.experimental.pallas import tpu as pltpu
from jax.sharding import PartitionSpec as P

MESH = pl.DeviceIdType.MESH
SIDE = 4
WIDTH = 4096
BLOCK = 16
CAPACITY = 4
CHOICES = 8
SLOTS = 64
ORDERS = (("x", "y", "z"), ("y", "z", "x"), ("z", "x", "y"))
WAVES = 2
PARTS = ORDERS * WAVES
WIDE = WIDTH + 256
TILES_OUT = (6, 6, 5)
TILES_BACK = (6, 6, 6, 5, 5, 4)
DIRECT_OUT = ((0, 0), (0, 1))
DIRECT_BACK = ((1, 1), (1, 2))
WIDEST = 768


def columns_of(tiles, part):
    return 128 * sum(tiles[:part]), 128 * tiles[part]


def my_place():
    row = lax.axis_index("dp")
    return {
        "y": row // (2 * SIDE),
        "x": (row // 2) % SIDE,
        "c": row % 2,
        "z": lax.axis_index("head"),
    }


def device_of(place):
    return ((place["y"] * SIDE + place["x"]) * 2 + place["c"], place["z"])


def shifted(place, axis, by):
    other = dict(place)
    other[axis] = (place[axis] + by) % SIDE
    return other


def sibling_of(place):
    other = dict(place)
    other["c"] = 1 - place["c"]
    return other


def greet(partners):
    barrier = pltpu.get_barrier_semaphore()
    for partner in partners:
        pl.semaphore_signal(barrier, inc=1, device_id=device_of(partner), device_id_type=MESH)
    pl.semaphore_wait(barrier, len(partners))


def remote(src, dst, send, recv, place):
    return pltpu.make_async_remote_copy(
        src_ref=src, dst_ref=dst, send_sem=send, recv_sem=recv,
        device_id=device_of(place), device_id_type=MESH,
    )


def blocks_at(ref, core, place, free, halves, columns):
    index = [core]
    last = max(free, key="zyx".index, default=None)
    for axis in ("z", "y", "x"):
        if axis in free:
            if halves is not None and axis == last:
                index.append(pl.ds(halves * (SIDE // 2), SIDE // 2))
            else:
                index.append(slice(None))
        else:
            index.append(place[axis])
    start, size = columns
    if not free and halves is not None:
        low = (size // 256) * 128
        start, size = (start, low) if halves == 0 else (start + low, size - low)
    return ref.at[(*index, slice(None), pl.ds(start, size))]


def attend_rows(base, rows, lengths_ref, query_ref, fresh_key_ref, fresh_value_ref, keys, values, attn_ref):
    slots, head_size = keys.shape[1:]
    heads = query_ref.shape[1] // head_size
    factor = 1.0 / math.sqrt(head_size)
    slot = lax.broadcasted_iota(jnp.int32, (heads, slots), 1)
    block = pl.ds(base, rows)
    query = jnp.stack([query_ref[block, head * head_size : (head + 1) * head_size].astype(jnp.float32) for head in range(heads)])
    query = jnp.swapaxes(query, 0, 1)
    narrow = query.astype(jnp.bfloat16)
    scores = []
    for row in range(rows):
        score = lax.dot_general(narrow[row], keys[base + row], (((1,), (1,)), ((), ())), preferred_element_type=jnp.float32)
        scores.append(jnp.where(slot < lengths_ref[base + row], score * factor, -1e30))
    scores = jnp.concatenate(scores, axis=0)
    fresh_key = fresh_key_ref[block].astype(jnp.float32).reshape(rows, 1, head_size)
    fresh = jnp.sum(query * fresh_key, axis=-1, keepdims=True).reshape(rows * heads, 1) * factor
    highest = jnp.maximum(jnp.max(scores, axis=-1, keepdims=True), fresh)
    spread = jnp.exp(scores - highest)
    fresh_exp = jnp.exp(fresh - highest)
    inverse = 1.0 / (jnp.sum(spread, axis=-1, keepdims=True) + fresh_exp)
    weights = (spread * inverse).astype(jnp.bfloat16)
    fresh_weight = (fresh_exp * inverse).astype(jnp.bfloat16).astype(jnp.float32)
    mixed = [
        jnp.dot(weights[row * heads : (row + 1) * heads], values[base + row], preferred_element_type=jnp.float32)
        for row in range(rows)
    ]
    fresh_value = fresh_value_ref[block].astype(jnp.float32).reshape(rows, 1, head_size)
    mixed = jnp.concatenate(mixed, axis=0).reshape(rows, heads, head_size) + fresh_weight.reshape(rows, heads, 1) * fresh_value
    mixed = jnp.swapaxes(mixed, 0, 1).astype(jnp.bfloat16)
    for head in range(heads):
        attn_ref[block, head * head_size : (head + 1) * head_size] = mixed[head]


def route_block(names_ref, names, weights, table):
    choices, rows = names.shape
    lane = lax.broadcasted_iota(jnp.int32, (choices, rows), 1)
    position = jnp.zeros((choices, rows), jnp.int32)
    for row in range(rows):
        same = names == names_ref[0, row]
        for choice in range(1, choices):
            same = same | (names == names_ref[choice, row])
        position += jnp.where(same & (lane > row), 1, 0)
    gates = weights / jnp.sum(weights, axis=0, keepdims=True)
    upper = gates.astype(jnp.bfloat16).astype(jnp.float32)
    table[...] = jnp.zeros_like(table)
    table[0:choices, 0:rows] = (names * CAPACITY + position).astype(jnp.float32)
    table[choices : 2 * choices, 0:rows] = upper
    table[2 * choices : 3 * choices, 0:rows] = gates - upper
    return table[...].T[0:rows].astype(jnp.bfloat16)


def attend_and_project_kernel(lengths_ref, names_ref, query_in, fresh_key_in, fresh_value_in, key_ref, value_ref,
                              weight_ref, residual_in, gain_in, names_in, weights_in, hidden_ref, normed_ref,
                              query_ref, fresh_key_ref, fresh_value_ref, residual_ref, gain_ref, names_here, weights_here, table,
                              attn_ref, keys, values, attn_all, weight_all, sums, sums_in, mine, mine_in,
                   local_sem, input_sem, key_sem, value_sem, w_send, w_recv, a_send, a_recv, f_send, f_recv, p_send, p_recv, s_send, s_recv, m_send, m_recv):
    me = my_place()
    sibling = sibling_of(me)
    rows, depth = attn_ref.shape
    inputs = [
        pltpu.make_async_copy(src, dst, input_sem.at[at])
        for at, (src, dst) in enumerate((
            (query_in, query_ref), (fresh_key_in, fresh_key_ref), (fresh_value_in, fresh_value_ref), (residual_in, residual_ref),
            (gain_in, gain_ref), (names_in, names_here), (weights_in, weights_here),
        ))
    ]
    for load in inputs:
        load.start()
    own_cols = weight_ref.shape[1]
    half_depth, half_rows = depth // 2, rows // 2
    step = 16
    loads = []
    for at in range(rows // step):
        block = pl.ds(at * step, step)
        loads.append((pltpu.make_async_copy(key_ref.at[block, 0], keys.at[block], key_sem.at[at]),
                      pltpu.make_async_copy(value_ref.at[block, 0], values.at[block], value_sem.at[at])))
        for load in loads[-1]:
            load.start()

    def neighbour(by, core):
        other = shifted(me, "x", by)
        other["c"] = (me["c"] + core) % 2
        return other

    others = [(by, core) for by in range(SIDE) for core in range(2) if by or core]
    greet([neighbour(*which) for which in others] + [shifted(me, axis, by) for axis in "yz" for by in (1, 2, 3)])

    def weight_at(by, low=0, size=depth):
        column = ((me["y"] + by) % SIDE) * own_cols
        return weight_all.at[pl.ds(low, size), pl.ds(pl.multiple_of(column, own_cols), own_cols)]

    def attn_at(by, core, low=0, size=rows):
        return attn_all.at[(me["x"] + by) % SIDE, core, pl.ds(low, size)]

    core = me["c"]
    own_w = pltpu.make_async_copy(weight_ref, weight_at(0), local_sem.at[0])
    own_w.start()
    started = []

    def go(src, dst, send, recv, place):
        copy = remote(src, dst, send, recv, place)
        copy.start()
        started.append(copy)
        return copy

    near_w, near_a, far_w, far_a, pair = {}, {}, {}, {}, {}
    for way, by in ((0, 1), (1, -1)):
        near_w[way] = go(weight_ref, weight_at(0), w_send.at[way], w_recv.at[way], shifted(me, "y", by))
    for load in inputs:
        load.wait()
    def send_attn(half):
        src, dst = attn_ref.at[pl.ds(half * half_rows, half_rows)], attn_at(0, core, half * half_rows, half_rows)
        for way, by in ((0, 1), (1, -1)):
            near_a[way, half] = go(src, dst, a_send.at[way, half], a_recv.at[way, half], shifted(me, "x", by))
        pair[0, half] = go(src, dst, p_send.at[0, half], p_recv.at[0, half], sibling)

    def pass_attn(way, by, half):
        near_a[way, half].wait_recv()
        block = attn_at(-by, core, half * half_rows, half_rows)
        if way == half:
            far_a[way] = go(block, block, f_send.at[way], f_recv.at[way], shifted(me, "x", by))
        pair[-by, half] = go(block, block, p_send.at[1 + way, half], p_recv.at[1 + way, half], sibling)

    chunks = rows // step
    for at in range(chunks):
        for load in loads[at]:
            load.wait()
        attend_rows(at * step, step, lengths_ref, query_ref, fresh_key_ref, fresh_value_ref, keys, values, attn_ref)
        if at == chunks // 2 - 1:
            send_attn(0)
    send_attn(1)
    own_a = pltpu.make_async_copy(attn_ref, attn_at(0, core), local_sem.at[1])
    own_a.start()
    for way, by in ((0, 1), (1, -1)):
        near_w[way].wait_recv()
        block = weight_at(-by, way * half_depth, half_depth)
        far_w[way] = go(block, block, w_send.at[2 + way], w_recv.at[2 + way], shifted(me, "y", by))
    for half in (0, 1):
        for way, by in ((0, 1), (1, -1)):
            pass_attn(way, by, half)
    for way in (0, 1):
        far_a[way].wait_recv()
        block = attn_at(2, core, way * half_rows, half_rows)
        pair[2, way] = go(block, block, p_send.at[3, way], p_recv.at[3, way], sibling)
    normed_ref[:, WIDTH : WIDTH + 128] = route_block(names_ref, names_here[...], weights_here[...], table)
    normed_ref[:, WIDTH + 128 :] = jnp.zeros((rows // SIDE, WIDE - WIDTH - 128), normed_ref.dtype)
    own_w.wait()
    own_a.wait()
    for way in (0, 1):
        far_w[way].wait_recv()

    share = rows // SIDE
    width = weight_all.shape[1]
    order = (0, 1, -1, 2)
    to_head = {}
    for number, by in enumerate(order):
        for half in (0, 1):
            pair[by, half].wait_recv()
        at = (me["x"] + by) % SIDE
        block = attn_all[at].reshape(2 * rows, depth)
        part = jnp.dot(block, weight_all[...], preferred_element_type=jnp.float32).astype(jnp.bfloat16)
        part = part.reshape(2, SIDE, share, width)
        for head in range(SIDE):
            sums[head, at] = part[:, head]
        for away in (1, 2, 3):
            target = shifted(me, "z", away)
            to_head[number, away] = go(sums.at[target["z"], at], sums_in.at[away - 1, at],
                                       s_send.at[number, away - 1], s_recv.at[number, away - 1], target)
    slots = {}
    for number, by in enumerate(order):
        at = (me["x"] + by) % SIDE
        for away in (1, 2, 3):
            to_head[number, away].wait_recv()
        total = sums[me["z"], at].astype(jnp.float32)
        for away in range(3):
            total += sums_in[away, at].astype(jnp.float32)
        mine[number] = total.astype(jnp.bfloat16)
        for flip in (0, 1):
            if by == 0 and flip == 0:
                continue
            target = neighbour(by, flip)
            slots[number, flip] = go(mine.at[number, target["c"]], mine_in.at[me["x"], core],
                                     m_send.at[number, flip], m_recv.at[number, flip], target)
    keep = pltpu.make_async_copy(mine.at[0, core], mine_in.at[me["x"], core], local_sem.at[2])
    keep.start()
    keep.wait()
    for copy in slots.values():
        copy.wait_recv()
    square = jnp.zeros((share, 1), jnp.float32)
    for y in range(SIDE):
        for x in range(SIDE):
            for c in range(2):
                start = ((y * SIDE + x) * 2 + c) * own_cols
                value = residual_ref[:, start : start + own_cols].astype(jnp.float32)
                value += mine_in[x, c, :, y * own_cols : (y + 1) * own_cols].astype(jnp.float32)
                hidden_ref[:, start : start + own_cols] = value
                square += jnp.sum(value * value, axis=-1, keepdims=True)
    scale = lax.rsqrt(square / WIDTH + 1e-06)
    for start in range(0, WIDTH, 512):
        normed_ref[:, start : start + 512] = (hidden_ref[:, start : start + 512] * scale * gain_ref[:, start : start + 512]).astype(jnp.bfloat16)
    for copy in started:
        copy.wait_send()


def attend_and_project(queries, new_keys, new_values, key_cache, value_cache, cache_lengths, out_weight, residual, gain, expert_ids, route_weights):
    rows, _, slots, head_size = key_cache.shape
    depth = queries.shape[1]
    own_cols = out_weight.shape[1]
    width = SIDE * own_cols
    share = rows // SIDE
    vmem, hbm, smem = (pl.BlockSpec(memory_space=space) for space in (pltpu.VMEM, pl.ANY, pltpu.SMEM))
    names, route_weights = expert_ids.T, route_weights.T
    bf16 = jnp.bfloat16
    dma = pltpu.SemaphoreType.DMA
    return pl.pallas_call(
        attend_and_project_kernel,
        out_shape=(
            jax.ShapeDtypeStruct((share, WIDTH), jnp.float32),
            jax.ShapeDtypeStruct((share, WIDE), bf16),
        ),
        in_specs=[smem, smem] + [hbm] * 10,
        out_specs=(vmem, vmem),
        scratch_shapes=[
            pltpu.VMEM((rows, depth), bf16),
            pltpu.VMEM(new_keys.shape, bf16),
            pltpu.VMEM(new_values.shape, bf16),
            pltpu.VMEM(residual.shape, bf16),
            pltpu.VMEM((1, WIDTH), jnp.float32),
            pltpu.VMEM(names.shape, jnp.int32),
            pltpu.VMEM(names.shape, jnp.float32),
            pltpu.VMEM((128, 128), jnp.float32),
            pltpu.VMEM((rows, depth), bf16),
            pltpu.VMEM((rows, slots, head_size), bf16),
            pltpu.VMEM((rows, slots, head_size), bf16),
            pltpu.VMEM((SIDE, 2, rows, depth), bf16),
            pltpu.VMEM((depth, width), bf16),
            pltpu.VMEM((SIDE, SIDE, 2, share, width), bf16),
            pltpu.VMEM((SIDE - 1, SIDE, 2, share, width), bf16),
            pltpu.VMEM((SIDE, 2, share, width), bf16),
            pltpu.VMEM((SIDE, 2, share, width), bf16),
            dma((3,)), dma((7,)), dma((rows // 16,)), dma((rows // 16,)),
            dma((4,)), dma((4,)), dma((2, 2)), dma((2, 2)), dma((2,)), dma((2,)), dma((4, 2)), dma((4, 2)),
            dma((4, 3)), dma((4, 3)), dma((4, 2)), dma((4, 2)),
        ],
        compiler_params=pltpu.CompilerParams(collective_id=3, has_side_effects=True, vmem_limit_bytes=60 * 1024 * 1024),
    )(cache_lengths, names, queries, new_keys, new_values, key_cache, value_cache, out_weight, residual, gain.reshape(1, WIDTH), names, route_weights)


def pick_group(table):
    span = table.shape[0]
    lane = lax.broadcasted_iota(jnp.int32, table.shape, 1)
    row = lax.broadcasted_iota(jnp.int32, (span, 1), 0)
    place = (row // BLOCK * CAPACITY).astype(jnp.float32)
    first = (lax.axis_index("dp") * 2 * CAPACITY).astype(jnp.float32)
    spot = lane.astype(jnp.float32)
    picked = jnp.zeros(table.shape, jnp.float32)
    gates = jnp.zeros(table.shape, jnp.float32)
    for own in range(2):
        code = table - (first + own * CAPACITY)
        hit = jnp.where((lane < CHOICES) & (code >= 0) & (code < CAPACITY), 1.0, 0.0)
        slot = jnp.sum(hit * (code + 1), axis=-1, keepdims=True)
        slot = jnp.where(slot > 0, slot - 1 + place + own * SLOTS, -1.0)
        gate = jnp.sum(table * (pltpu.roll(hit, CHOICES, 1) + pltpu.roll(hit, 2 * CHOICES, 1)), axis=-1, keepdims=True)
        match = spot == slot
        picked += jnp.where(match, 1.0, 0.0)
        gates += jnp.where(match, gate, 0.0)
    scale = jnp.broadcast_to(jnp.sum(gates, axis=0, keepdims=True), (128, 128)).T
    return picked, scale


def open_kernel(mine_ref, gate_ref, up_ref, act_ref, pick_ref, everyone, gate_w, up_w, chosen, scales, gate_sum, up_sum,
                own_sem, weight_sem, near_send, near_recv, far_send, far_recv, pair_send, pair_recv, first_send, first_recv):
    me = my_place()
    core = me["c"]
    sibling = sibling_of(me)
    loads = [pltpu.make_async_copy(gate_ref, gate_w, weight_sem.at[0]), pltpu.make_async_copy(up_ref, up_w, weight_sem.at[1])]
    greet([sibling] + [shifted(me, axis, by) for axis in "xyz" for by in (1, 2, 3)])
    home = everyone.at[core, me["z"], me["y"], me["x"]]
    own = pltpu.make_async_copy(mine_ref, home, own_sem)
    own.start()
    first = remote(mine_ref, home, first_send, first_recv, sibling)
    first.start()
    own.wait()
    first.wait_recv()
    near, far, pair = {}, {}, {}

    def group(part, stage, coordinate_shift, halves=None):
        order = PARTS[part]
        place = shifted(me, order[stage], coordinate_shift)
        start, size = columns_of(TILES_OUT, part % 3)
        start = pl.multiple_of(core * (WIDE // 2) + start, 128)
        return blocks_at(everyone, part // 3, place, order[:stage], halves, (start, size))

    def to_pair(part, stage, number, block):
        copy = remote(block, block, pair_send.at[part, stage, number], pair_recv.at[part, stage, number], sibling)
        copy.start()
        pair[part, stage, number] = copy

    def send_near(wave, stage):
        for part in range(3 * wave, 3 * wave + 3):
            block = group(part, stage, 0)
            if (wave, stage) in DIRECT_OUT:
                copy = remote(block, block, far_send.at[part, stage, 0], far_recv.at[part, stage, 0], shifted(me, PARTS[part][stage], 2))
                copy.start()
                far[part, stage, 0] = copy
            for way, by in ((0, 1), (1, -1)):
                copy = remote(block, block, near_send.at[part, stage, way], near_recv.at[part, stage, way], shifted(me, PARTS[part][stage], by))
                copy.start()
                near[part, stage, way] = copy

    def send_far(wave, stage):
        for part in range(3 * wave, 3 * wave + 3):
            for way, by in ((0, 1), (1, -1)):
                near[part, stage, way].wait_recv()
                if (wave, stage) not in DIRECT_OUT:
                    block = group(part, stage, -by, way)
                    copy = remote(block, block, far_send.at[part, stage, way], far_recv.at[part, stage, way], shifted(me, PARTS[part][stage], by))
                    copy.start()
                    far[part, stage, way] = copy
                to_pair(part, stage, way, group(part, stage, -by))

    def take_far(wave, stage):
        for part in range(3 * wave, 3 * wave + 3):
            for way in (0, 1):
                if (part, stage, way) in far:
                    far[part, stage, way].wait_recv()
            to_pair(part, stage, 2, group(part, stage, 2))

    groups, span = pick_ref.shape[0], pick_ref.shape[1]

    def choose(at, _):
        c, z = at // SIDE, at % SIDE
        picked, scale = pick_group(everyone[c, z, :, :, :, WIDTH : WIDTH + 128].reshape(span, 128).astype(jnp.float32))
        pick_ref[at] = picked.astype(jnp.bfloat16)
        turned = picked.T.astype(jnp.bfloat16)
        for half in range(2):
            scales[half, at] = scale[half * SLOTS : half * SLOTS + SLOTS]
        for start in range(0, WIDTH, 512):
            rows = everyone[c, z, :, :, :, start : start + 512].reshape(span, 512)
            part = jnp.dot(turned, rows, preferred_element_type=jnp.float32).astype(jnp.bfloat16)
            for half in range(2):
                chosen[half, at, :, start : start + 512] = part[half * SLOTS : half * SLOTS + SLOTS]
        return 0

    depth = 1024
    share = groups // 2

    def open_one(wave, own):
        gate_sum[...] = jnp.zeros_like(gate_sum)
        up_sum[...] = jnp.zeros_like(up_sum)

        def multiply(step, _):
            columns = pl.ds(pl.multiple_of(step * depth, depth), depth)
            rows = chosen[own, wave * share : (wave + 1) * share, :, columns].reshape(share * SLOTS, depth)
            gate_sum[...] += jnp.dot(rows, gate_w[own, columns, :], preferred_element_type=jnp.float32)
            up_sum[...] += jnp.dot(rows, up_w[own, columns, :], preferred_element_type=jnp.float32)
            return 0

        lax.fori_loop(0, WIDTH // depth, multiply, 0)

        def finish(at, _):
            rows = pl.ds(pl.multiple_of(at * SLOTS, SLOTS), SLOTS)
            value = gate_sum[rows]
            there = pl.ds(pl.multiple_of((wave * share + at) * SLOTS, SLOTS), SLOTS)
            act_ref[own, there] = (value / (1.0 + jnp.exp(-value)) * up_sum[rows] * scales[own, wave * share + at][:, :1]).astype(jnp.bfloat16)
            return 0

        lax.fori_loop(0, share, finish, 0)

    def settle(wave):
        for (part, _, _), copy in pair.items():
            if part // 3 == wave:
                copy.wait_recv()
        lax.fori_loop(wave * share, (wave + 1) * share, choose, 0)

    send_near(0, 0)
    send_near(1, 0)
    for load in loads:
        load.start()
    send_far(0, 0)
    take_far(0, 0)
    send_near(0, 1)
    send_far(1, 0)
    take_far(1, 0)
    send_near(1, 1)
    send_far(0, 1)
    take_far(0, 1)
    send_near(0, 2)
    send_far(1, 1)
    take_far(1, 1)
    send_far(0, 2)
    send_near(1, 2)
    take_far(0, 2)
    settle(0)
    send_far(1, 2)
    for load in loads:
        load.wait()
    open_one(0, 0)
    open_one(0, 1)
    take_far(1, 2)
    settle(1)
    open_one(1, 0)
    open_one(1, 1)
    for copy in [first, *near.values(), *far.values(), *pair.values()]:
        copy.wait_send()


def gather_and_open(mine, w_gate, w_up):
    bf16, f32, dma = jnp.bfloat16, jnp.float32, pltpu.SemaphoreType.DMA
    groups, span = 2 * SIDE, SIDE * SIDE * BLOCK
    hidden = w_gate.shape[2]
    vmem, hbm = pl.BlockSpec(memory_space=pltpu.VMEM), pl.BlockSpec(memory_space=pl.ANY)
    parts = len(PARTS)
    return pl.pallas_call(
        open_kernel,
        out_shape=(
            jax.ShapeDtypeStruct((2, groups * SLOTS, hidden), bf16),
            jax.ShapeDtypeStruct((groups, span, 128), bf16),
        ),
        in_specs=[vmem, hbm, hbm],
        out_specs=(vmem, vmem),
        scratch_shapes=[
            pltpu.VMEM((2, SIDE, SIDE, SIDE, *mine.shape), bf16),
            pltpu.VMEM(w_gate.shape, bf16),
            pltpu.VMEM(w_up.shape, bf16),
            pltpu.VMEM((2, groups, SLOTS, WIDTH), bf16),
            pltpu.VMEM((2, groups, SLOTS, 128), f32),
            pltpu.VMEM((groups // 2 * SLOTS, hidden), f32),
            pltpu.VMEM((groups // 2 * SLOTS, hidden), f32),
            dma, dma((2,)),
            dma((parts, 3, 2)), dma((parts, 3, 2)), dma((parts, 3, 2)), dma((parts, 3, 2)),
            dma((parts, 3, 3)), dma((parts, 3, 3)), dma, dma,
        ],
        compiler_params=pltpu.CompilerParams(collective_id=1, has_side_effects=True, vmem_limit_bytes=60 * 1024 * 1024),
    )(mine, w_gate, w_up)

def close_kernel(act_ref, pick_ref, down_ref, out_ref, acc, pair_buf, down_w, result,
                 near0, near1, near2, far0, far1, far2,
                 weight_sem, pair_send, pair_recv, near_send, near_recv, far_send, far_recv):
    me = my_place()
    core = me["c"]
    sibling = sibling_of(me)
    near_bufs, far_bufs = (near0, near1, near2), (far0, far1, far2)
    loads = []
    for part in range(len(PARTS)):
        start, size = columns_of(TILES_BACK, part)
        columns = (slice(None), slice(None), pl.ds(start, size))
        loads.append(pltpu.make_async_copy(down_ref.at[columns], down_w.at[columns], weight_sem.at[part]))
        loads[-1].start()
    greet([sibling] + [shifted(me, axis, by) for axis in "xyz" for by in (1, 2, 3)])
    pair, near, far = {}, {}, {}
    groups, span = pick_ref.shape[0], pick_ref.shape[1]

    def axis_of(part, stage):
        return PARTS[part][2 - stage]

    def group(ref, part, stage, shift, which, halves=None):
        place = shifted(me, axis_of(part, stage), shift)
        return blocks_at(ref, which, place, PARTS[part][: 2 - stage], halves, columns_of(TILES_BACK, part))

    def multiply(part):
        loads[part].wait()
        start, size = columns_of(TILES_BACK, part)
        for own in range(2):
            product = jnp.dot(act_ref[own], down_w[own, :, start : start + size], preferred_element_type=jnp.float32)
            result[:, own, :, :size] = product.astype(jnp.bfloat16).reshape(groups, SLOTS, size)

        def spread(at, _):
            both = result[at, :, :, :size].reshape(2 * SLOTS, size)
            rows = jnp.dot(pick_ref[at], both, preferred_element_type=jnp.float32).astype(jnp.bfloat16)
            acc[at // SIDE, at % SIDE, :, :, :, start : start + size] = rows.reshape(SIDE, SIDE, BLOCK, size)
            return 0

        lax.fori_loop(0, groups, spread, 0)
        for number, shift in enumerate((2, 1, -1, 0)):
            copy = remote(
                group(acc, part, 0, shift, 1 - core), group(pair_buf, part, 0, shift, 0),
                pair_send.at[part, number], pair_recv.at[part, number], sibling,
            )
            copy.start()
            pair[part, number] = copy

    def add_into(target, others):
        lead = target.shape[:-2]
        count = math.prod(lead)

        def body(at, _):
            index = []
            rest = at
            for size in reversed(lead):
                index.insert(0, rest % size)
                rest = rest // size
            index = (*index, slice(None), slice(None))
            total = target[index].astype(jnp.float32)
            for other in others:
                total += other[index].astype(jnp.float32)
            target[index] = total.astype(target.dtype)
            return 0

        if count == 1:
            body(0, 0)
        else:
            lax.fori_loop(0, count, body, 0)

    def add_pair(part, number, shift):
        pair[part, number].wait_recv()
        add_into(group(acc, part, 0, shift, core), [group(pair_buf, part, 0, shift, 0)])

    def near_copy(part, stage, way, half):
        by = 1 if way == 0 else -1
        src = group(acc, part, stage, by, core, half)
        dst = near_bufs[stage].at[part, way, half, ..., pl.ds(0, src.shape[-1])]
        copy = remote(src, dst, near_send.at[part, stage, way, half], near_recv.at[part, stage, way, half], shifted(me, axis_of(part, stage), by))
        copy.start()
        near[part, stage, way, half] = copy

    def send_far(wave, stage, parts=range(3)):
        for part in (3 * wave + at for at in parts):
            if stage == 0:
                add_pair(part, 0, 2)
            for way, by in ((0, 1), (1, -1)):
                src = group(acc, part, stage, 2, core, way)
                dst = far_bufs[stage].at[part, way, ..., pl.ds(0, src.shape[-1])]
                by = 2 if (wave, stage) in DIRECT_BACK else by
                copy = remote(src, dst, far_send.at[part, stage, way], far_recv.at[part, stage, way], shifted(me, axis_of(part, stage), by))
                copy.start()
                far[part, stage, way] = copy

    def send_near(wave, stage, parts=range(3)):
        for part in (3 * wave + at for at in parts):
            for way, by in ((0, 1), (1, -1)):
                if stage == 0:
                    add_pair(part, 1 + way, by)
                near_copy(part, stage, way, 1 - way)
                if (wave, stage) in DIRECT_BACK:
                    near_copy(part, stage, way, way)

    def relay(wave, stage):
        if (wave, stage) in DIRECT_BACK:
            return
        for part in range(3 * wave, 3 * wave + 3):
            for way, by in ((0, 1), (1, -1)):
                far[part, stage, way].wait_recv()
                target = group(acc, part, stage, by, core, way)
                add_into(target, [far_bufs[stage].at[part, way, ..., pl.ds(0, target.shape[-1])]])
                near_copy(part, stage, way, way)

    def take(wave, stage):
        for part in range(3 * wave, 3 * wave + 3):
            if stage == 0:
                add_pair(part, 3, 0)
            for half in (0, 1):
                for way in (0, 1):
                    near[part, stage, way, half].wait_recv()
                target = group(acc, part, stage, 0, core, half)
                others = [near_bufs[stage].at[part, way, half, ..., pl.ds(0, target.shape[-1])] for way in (0, 1)]
                if (wave, stage) in DIRECT_BACK:
                    far[part, stage, half].wait_recv()
                    others.append(far_bufs[stage].at[part, half, ..., pl.ds(0, target.shape[-1])])
                if stage < 2:
                    add_into(target, others)
                else:
                    total = target[...].astype(jnp.float32)
                    for other in others:
                        total += other[...].astype(jnp.float32)
                    start, size = columns_of(TILES_BACK, part)
                    low = (size // 256) * 128
                    start, size = (start, low) if half == 0 else (start + low, size - low)
                    out_ref[:, pl.ds(start, size)] = total

    multiply(0)
    multiply(1)
    send_far(0, 0, (0,))
    multiply(2)
    send_far(0, 0, (1,))
    send_near(0, 0, (0,))
    send_far(0, 0, (2,))
    send_near(0, 0, (1, 2))
    for part in range(3, 6):
        multiply(part)
    relay(0, 0)
    send_far(1, 0)
    send_near(1, 0)
    take(0, 0)
    send_far(0, 1)
    send_near(0, 1)
    relay(1, 0)
    relay(0, 1)
    take(0, 1)
    send_far(0, 2)
    send_near(0, 2)
    take(1, 0)
    send_far(1, 1)
    send_near(1, 1)
    relay(0, 2)
    relay(1, 1)
    take(0, 2)
    take(1, 1)
    send_far(1, 2)
    send_near(1, 2)
    relay(1, 2)
    take(1, 2)
    for copy in [*pair.values(), *near.values(), *far.values()]:
        copy.wait_send()


def close_and_reduce(act, pick, w_down):
    bf16, dma = jnp.bfloat16, pltpu.SemaphoreType.DMA
    groups = pick.shape[0]
    half = SIDE // 2
    parts = len(PARTS)
    last = WIDEST // 2
    vmem, hbm = pl.BlockSpec(memory_space=pltpu.VMEM), pl.BlockSpec(memory_space=pl.ANY)
    return pl.pallas_call(
        close_kernel,
        out_shape=jax.ShapeDtypeStruct((BLOCK, WIDTH), jnp.float32),
        in_specs=[vmem, vmem, hbm],
        out_specs=vmem,
        scratch_shapes=[
            pltpu.VMEM((2, SIDE, SIDE, SIDE, BLOCK, WIDTH), bf16),
            pltpu.VMEM((1, SIDE, SIDE, SIDE, BLOCK, WIDTH), bf16),
            pltpu.VMEM(w_down.shape, bf16),
            pltpu.VMEM((groups, 2, SLOTS, WIDEST), bf16),
            pltpu.VMEM((parts, 2, 2, SIDE, half, BLOCK, WIDEST), bf16),
            pltpu.VMEM((parts, 2, 2, half, BLOCK, WIDEST), bf16),
            pltpu.VMEM((parts, 2, 2, BLOCK, last), bf16),
            pltpu.VMEM((parts, 2, SIDE, half, BLOCK, WIDEST), bf16),
            pltpu.VMEM((parts, 2, half, BLOCK, WIDEST), bf16),
            pltpu.VMEM((parts, 2, BLOCK, last), bf16),
            dma((parts,)), dma((parts, 4)), dma((parts, 4)),
            dma((parts, 3, 2, 2)), dma((parts, 3, 2, 2)), dma((parts, 3, 2)), dma((parts, 3, 2)),
        ],
        compiler_params=pltpu.CompilerParams(collective_id=2, has_side_effects=True, vmem_limit_bytes=60 * 1024 * 1024),
    )(act, pick, w_down)


def on_device(
    queries,
    new_keys,
    new_values,
    key_cache,
    value_cache,
    cache_lengths,
    out_weight,
    residual_in,
    norm_gain,
    expert_ids,
    route_weights,
    w_gate,
    w_up,
    w_down,
):
    hidden_one, normed = attend_and_project(
        queries, new_keys, new_values, key_cache, value_cache, cache_lengths, out_weight, residual_in, norm_gain,
        expert_ids, route_weights,
    )
    act, pick = gather_and_open(normed, w_gate, w_up)
    return (hidden_one + close_and_reduce(act, pick, w_down)).astype(jnp.bfloat16)


def solution(mesh):
    in_specs = (
        P("dp", "head"),
        P("dp", "head"),
        P("dp", "head"),
        P("dp", "head", None, None),
        P("dp", "head", None, None),
        P("dp"),
        P("head", "dp"),
        P(("dp", "head"), None),
        P(),
        P(("dp", "head"), None),
        P(("dp", "head"), None),
        P("dp", None, "head"),
        P("dp", None, "head"),
        P("dp", "head", None),
    )
    out_specs = P(("dp", "head"), None)
    return jax.shard_map(
        on_device, mesh=mesh, in_specs=in_specs, out_specs=out_specs, check_vma=False
    )
```
